32 devices in a mesh: spec: 4 (over x, core), neuron: 8 (over z, y).
Axes of the slice: x: 2, y: 2, z: 4, core: 2. Of those that a mesh axis runs over, the one named last changes fastest.
Arguments:
- center: float32 [32, 8192], P('spec', 'neuron'), may hold values from -6 to 6
- radius: float32 [32, 8192], P('spec', 'neuron'), may hold values from 0.002 to 0.02
- weight: float32 [4096, 8192], P('neuron'), may hold values from -0.0625 to 0.0625
- bias: float32 [4096], P('neuron'), may hold values from -3 to 3
- out_weight: float32 [1000, 4096], P(None, 'neuron'), may hold values from -0.09375 to 0.09375
- masks: int32 [32, 4096], P(None, 'neuron'), may hold values from 0 to 2
- image_labels: int32 [32], replicated, may hold values from 0 to 999
- runner_up: int32 [2048], P('spec'), may hold values from 0 to 999
- spec_image: int32 [2048], P('spec'), may hold values from 0 to 31
Outputs:
- input_coeffs: float32 [2048, 8192], P('spec', 'neuron')
- margin_bounds: float32 [2048], P('spec')
The draws below stay inside these ranges and needn't reach their ends.
All inputs are finite; a program needn't handle non-finite values.
Results may differ from the reference program's by a relative error of at most 0.000098.
Values sent between devices are 32-bit elements; how exact they have to be, the bound alone decides.
No kernel may reach another device: no remote copies, remote signals or barrier semaphores. Data moves between devices by JAX's collectives and lax.ppermute only.
A program may use at most 128 MiB of HBM per device.

```python
import math
import jax
import jax.numpy as jnp
from jax import lax

D = 8192
H = 4096
CLASSES = 1000
B_TOTAL = 32
SPECS = 2048


def touch_ends(drawn, stream_key, smallest, high):
    longest = drawn.shape.index(max(drawn.shape))
    spots = []
    for shift in (0, 1):
        where = [jax.random.randint(jax.random.fold_in(stream_key, axis), (), 0, length) for axis, length in enumerate(drawn.shape)]
        where[longest] = (where[longest] + shift) % drawn.shape[longest]
        spots.append(tuple(where))
    return drawn.at[spots[0]].set(smallest).at[spots[1]].set(high)


def steps_of(key, dims, pieces, smallest, top_value):
    def one(axis_at, blocks):
        steps = jax.random.uniform(jax.random.fold_in(jax.random.fold_in(key, 6), axis_at), (blocks,), jnp.float32, smallest / len(pieces), top_value / len(pieces))
        return jnp.repeat(jnp.exp(steps), dims[axis_at] // blocks).reshape((-1,) + (1,) * (len(dims) - axis_at - 1))

    loudness = one(*pieces[0])
    for cut in pieces[1:]:
        loudness = loudness * one(*cut)
    return loudness


def gaussian(rng, dims, spread, bound, shards=(), kind=jnp.bfloat16):
    result = spread * jax.random.normal(rng, dims, jnp.float32)
    if shards:
        result = result * steps_of(rng, dims, shards, -0.22, 0.18)
    return jnp.clip(result, -bound, bound).astype(kind)


def setup_inputs(seed: int = 0) -> dict:
    splits = jax.random.split(jax.random.key(seed), 10)
    return {
        "center": gaussian(splits[0], (B_TOTAL, D), 1.0, 6.0, ((0, 4), (1, 8)), jnp.float32),
        "radius": jnp.clip(jnp.exp(math.log(0.02) - 2.30258502 * jax.random.uniform(splits[1], (B_TOTAL, D), jnp.float32) ** steps_of(splits[1], (B_TOTAL, D), ((0, 4), (1, 8)), -0.2, 0.2)), 0.002, 0.02),
        "weight": gaussian(splits[2], (H, D), D ** -0.5, 0.0625, ((0, 8),), jnp.float32),
        "bias": gaussian(splits[3], (H,), 0.5, 3.0, ((0, 8),), jnp.float32),
        "out_weight": gaussian(splits[4], (CLASSES, H), H ** -0.5, 0.09375, ((1, 8),), jnp.float32),
        "masks": touch_ends(jax.random.randint(splits[5], (B_TOTAL, H), 0, 3), jax.random.fold_in(splits[5], 1), 0, 2).astype(jnp.int32),
        "image_labels": touch_ends(jax.random.randint(splits[6], (B_TOTAL,), 0, CLASSES), jax.random.fold_in(splits[6], 1), 0, CLASSES - 1).astype(jnp.int32),
        "runner_up": touch_ends(jax.random.randint(splits[7], (SPECS,), 0, CLASSES), jax.random.fold_in(splits[7], 1), 0, CLASSES - 1).astype(jnp.int32),
        "spec_image": touch_ends(jax.random.randint(splits[8], (SPECS,), 0, B_TOTAL), jax.random.fold_in(splits[8], 1), 0, B_TOTAL - 1).astype(jnp.int32),
    }


def relax(pre_center, pre_radius, masks):
    upper = pre_center + pre_radius
    lower = pre_center - pre_radius
    slope = jnp.clip(upper / (upper - lower), 0.0, 1.0)
    slopes = jnp.where(masks == 1, jnp.ones_like(slope), jnp.where(masks == 2, slope, jnp.zeros_like(slope)))
    offsets = jnp.where(masks == 2, slope * lower, jnp.zeros_like(slope))
    return slopes, offsets


def reference(center, radius, weight, bias, out_weight, masks, image_labels, runner_up, spec_image):
    highest = lax.Precision.HIGHEST
    pre_center = jnp.dot(center, weight.T, precision=highest) + bias
    pre_radius = jnp.dot(radius, jnp.abs(weight).T, precision=highest)
    slopes, offsets = relax(pre_center, pre_radius, masks)
    true_class = image_labels[spec_image]
    spec_coeff = out_weight[true_class] - out_weight[runner_up]
    scaled = spec_coeff * slopes[spec_image]
    relax_term = -jnp.sum(jnp.minimum(spec_coeff, 0.0) * offsets[spec_image], axis=1) + jnp.sum(scaled * bias, axis=1)
    input_coeffs = jnp.dot(scaled, weight, precision=highest)
    input_term = jnp.sum(input_coeffs * center[spec_image] - jnp.abs(input_coeffs) * radius[spec_image], axis=1)
    return input_coeffs, input_term + relax_term
```

```python
import functools

import jax
import jax.numpy as jnp
from jax import lax
from jax.sharding import PartitionSpec as P

GROUP = 4
HIGH = lax.Precision.HIGH


def swap(array, axis, size, k):
    return lax.ppermute(array, axis, [(i, i ^ k) for i in range(size)])


def local(members, sites, center, radius, weight, bias, out_weight, masks, image_labels, runner_up, spec_image):
    g, n = lax.axis_index("spec"), lax.axis_index("neuron")
    q = g % GROUP
    rows, cols = weight.shape[0], center.shape[1]
    images, specs, classes = center.shape[0], spec_image.shape[0], out_weight.shape[0]
    piece = cols // GROUP
    far = sites // GROUP
    over_spec = functools.partial(swap, axis="spec", size=members)
    over_neuron = functools.partial(swap, axis="neuron", size=sites)

    boxes = jnp.stack([center, radius])
    boxes_by_site = [boxes] + [over_neuron(boxes, k=k) for k in range(1, sites)]

    share = -(-classes // GROUP // 8) * 8
    starts = jnp.minimum(jnp.arange(GROUP) * share, classes - share)
    own = lax.dynamic_slice(out_weight, (starts[q], 0), (share, rows))
    two = over_neuron(own, k=2)
    one = over_neuron(own, k=1)
    three = over_neuron(two, k=1)
    shares = jnp.stack([one, two, three])
    s2 = over_spec(shares, k=2)
    s1 = over_spec(shares, k=1)
    s3 = over_spec(s2, k=1)
    ow_parts = [shares, s1, s2, s3]

    def columns(block, quarter):
        return lax.dynamic_slice(weight, (0, block * cols + quarter * piece), (rows, piece))

    def weight_parts(da):
        home = jnp.stack([over_neuron(columns(n ^ j ^ (GROUP * da), q), k=j) for j in range(1, GROUP)])
        w2 = over_spec(home, k=2)
        w1 = over_spec(home, k=1)
        w3 = over_spec(w2, k=1)
        got = [home, w1, w2, w3]
        return [
            jnp.concatenate([columns(n ^ (GROUP * da), q ^ r), got[r].reshape(-1, piece)]) for r in range(GROUP)
        ]

    full = jnp.take(jnp.stack(boxes_by_site), n ^ jnp.arange(sites), axis=0)
    full = full.transpose(1, 2, 0, 3).reshape(2, images, sites * cols)
    dims = (((1,), (1,)), ((), ()))
    pre_center = lax.dot_general(full[0], weight, dims, precision=HIGH) + bias
    pre_radius = lax.dot_general(full[1], jnp.abs(weight), dims, precision=HIGH)
    mask = lax.dynamic_slice(masks, (g * images, 0), (images, rows))
    upper, lower = pre_center + pre_radius, pre_center - pre_radius
    slope = jnp.clip(upper / (upper - lower), 0.0, 1.0)
    slopes = jnp.where(mask == 1, 1.0, jnp.where(mask == 2, slope, 0.0))
    offsets = jnp.where(mask == 2, slope * lower, 0.0)
    both = jnp.stack([slopes, offsets])
    both = jnp.concatenate([both] + [over_spec(both, k=r) for r in range(1, members)], axis=1)
    slopes_here, offsets_here = both[0], both[1]
    slopes_parts = [slopes_here] + [over_neuron(slopes_here, k=j) for j in range(1, GROUP)]

    image_at = ((spec_image // images) ^ g) * images + spec_image % images
    pick_image = (image_at[:, None] == jnp.arange(members * images)).astype(jnp.float32)
    true_class = jnp.take(image_labels, spec_image, axis=0)
    klass = jnp.arange(classes)
    pick = (true_class[:, None] == klass).astype(jnp.float32) - (runner_up[:, None] == klass).astype(jnp.float32)

    def place(label):
        part = label // share
        return (part ^ q) * share + label - starts[part]

    spot = jnp.arange(GROUP * share)
    pick_rel = (place(true_class)[:, None] == spot).astype(jnp.float32) - (
        place(runner_up)[:, None] == spot
    ).astype(jnp.float32)
    spec_coeff = jnp.dot(pick, out_weight, precision=HIGH)
    scaled = [spec_coeff * jnp.dot(pick_image, slopes_parts[0], precision=HIGH)]
    for j in range(1, GROUP):
        ow = jnp.concatenate([part[j - 1] for part in ow_parts])
        scaled.append(jnp.dot(pick_rel, ow, precision=HIGH) * jnp.dot(pick_image, slopes_parts[j], precision=HIGH))
    offset_rows = jnp.dot(pick_image, offsets_here, precision=HIGH)
    relax_part = jnp.sum(scaled[0] * bias - jnp.minimum(spec_coeff, 0.0) * offset_rows, axis=1)
    scaled = jnp.concatenate(scaled, axis=1)

    total = [None] * GROUP
    for da in list(range(1, far)) + [0]:
        for r, part in enumerate(weight_parts(da)):
            got = jnp.dot(scaled, part, precision=HIGH)
            if da:
                got = over_neuron(got, k=GROUP * da)
            total[r] = got if total[r] is None else total[r] + got
    input_coeffs = jnp.take(jnp.stack(total), q ^ jnp.arange(GROUP), axis=0)
    input_coeffs = input_coeffs.transpose(1, 0, 2).reshape(specs, cols)

    near = jnp.concatenate([boxes] + [over_spec(boxes, k=r) for r in range(1, members)], axis=1)
    center_rows = jnp.dot(pick_image, near[0], precision=lax.Precision.HIGHEST)
    radius_rows = jnp.dot(pick_image, near[1], precision=lax.Precision.HIGHEST)
    margin = jnp.sum(input_coeffs * center_rows - jnp.abs(input_coeffs) * radius_rows, axis=1) + relax_part
    k = 1
    while k < sites:
        margin = margin + over_neuron(margin, k=k)
        k *= 2
    return input_coeffs, margin


def solution(mesh):
    members, sites = mesh.shape["spec"], mesh.shape["neuron"]
    return jax.shard_map(
        functools.partial(local, members, sites),
        mesh=mesh,
        in_specs=(
            P("spec", "neuron"),
            P("spec", "neuron"),
            P("neuron", None),
            P("neuron"),
            P(None, "neuron"),
            P(None, "neuron"),
            P(),
            P("spec"),
            P("spec"),
        ),
        out_specs=(P("spec", "neuron"), P("spec")),
        check_vma=False,
    )
```

```python
import functools

import jax
import jax.numpy as jnp
from jax import lax
from jax.experimental import pallas as pl
from jax.experimental.pallas import tpu as pltpu
from jax.sharding import PartitionSpec as P

QUARTERS = 4
F32, BF16 = jnp.float32, jnp.bfloat16
ROWS = (((1,), (0,)), ((), ()))
BOTH = (((1,), (1,)), ((), ()))


def swap(array, axis, size, k):
    return lax.ppermute(array, axis, [(i, i ^ k) for i in range(size)])


def in_order(*values):
    return lax.optimization_barrier(values)


def dot(a, b, dims=ROWS):
    return lax.dot_general(a, b, dims, preferred_element_type=F32)


def two_terms(x):
    high = x.astype(BF16)
    return high, (x - high.astype(F32)).astype(BF16)


def three_terms(x):
    high, rest = x.astype(BF16), None
    rest = x - high.astype(F32)
    middle = rest.astype(BF16)
    return high, middle, (rest - middle.astype(F32)).astype(BF16)


def one_hot(index, size):
    return (index == lax.broadcasted_iota(jnp.int32, (index.shape[0], size), 1)).astype(F32)


def row_sums(x):
    ones = jnp.ones((8, x.shape[1]), BF16)
    return sum(dot(ones, term, BOTH) for term in three_terms(x))


def scale_kernel(parts, with_relax, at_ref, *refs):
    ow_refs, slopes_ref = refs[:parts], refs[parts]
    rest = refs[parts + 1 :]
    at = at_ref[...]
    first = 3 if with_relax else 0
    size = sum(ref.shape[0] for ref in ow_refs)
    pick = (one_hot(at[:, first : first + 1], size) - one_hot(at[:, first + 1 : first + 2], size)).astype(BF16)
    coeff, low = None, 0
    for ref in ow_refs:
        here = pick[:, low : low + ref.shape[0]]
        low += ref.shape[0]
        high_ow, low_ow = two_terms(ref[...])
        got = dot(here, high_ow) + dot(here, low_ow)
        coeff = got if coeff is None else coeff + got
    image = one_hot(at[:, 2:3], slopes_ref.shape[0]).astype(BF16)
    scaled = coeff * sum(dot(image, term) for term in three_terms(slopes_ref[...]))
    if with_relax:
        offsets_ref, bias_ref, high_ref, low_ref, relax_ref = rest
        offsets = sum(dot(image, term) for term in three_terms(offsets_ref[...]))
        relax_ref[...] = row_sums(scaled * bias_ref[...] - jnp.minimum(coeff, 0.0) * offsets)
    else:
        high_ref, low_ref = rest
    high_ref[...], low_ref[...] = two_terms(scaled)


def scale(at, ow_parts, slopes, offsets=None, bias=None):
    specs, rows = at.shape[0], slopes.shape[1]
    with_relax = offsets is not None
    outs = [jax.ShapeDtypeStruct((specs, rows), BF16)] * 2
    extra = []
    if with_relax:
        outs = outs + [jax.ShapeDtypeStruct((8, specs), F32)]
        extra = [offsets, bias]
    size = sum(part.shape[0] for part in ow_parts)
    return pl.pallas_call(
        functools.partial(scale_kernel, len(ow_parts), with_relax),
        out_shape=outs,
        compiler_params=pltpu.CompilerParams(vmem_limit_bytes=40 * 2**20),
        cost_estimate=pl.CostEstimate(
            flops=4 * specs * size * rows, bytes_accessed=4 * size * rows + 4 * specs * rows, transcendentals=0
        ),
    )(at, *ow_parts, slopes, *extra)


def product_kernel(group, final, col_ref, *refs):
    scaled_refs, w_refs = refs[: 2 * group], refs[2 * group : 3 * group]
    rest = refs[3 * group :]
    w_high, w_low = rest[-2:]
    rows = w_refs[0].shape[0]

    @pl.when(pl.program_id(0) == 0)
    def _():
        for j, ref in enumerate(w_refs):
            w_high[pl.ds(j * rows, rows), :], w_low[pl.ds(j * rows, rows), :] = two_terms(ref[...])

    total = None
    for j in range(group):
        high, low = scaled_refs[2 * j][...], scaled_refs[2 * j + 1][...]
        wh, wl = w_high[pl.ds(j * rows, rows), :], w_low[pl.ds(j * rows, rows), :]
        got = dot(high, wh) + (dot(high, wl) + dot(low, wh))
        total = got if total is None else total + got
    if not final:
        rest[0][...] = total
        return
    sums, near = final
    sum_refs, (at_ref, center_ref, radius_ref, margin_in), (out_ref, margin_ref) = (
        rest[:sums],
        rest[sums : sums + 4],
        rest[-4:-2],
    )
    for ref in sum_refs:
        total = total + ref[...]
    out_ref[...] = total
    image = one_hot(at_ref[...][:, 2:3], near).astype(BF16)
    center = sum(dot(image, term) for term in three_terms(center_ref[...]))
    radius = sum(dot(image, term) for term in three_terms(radius_ref[...]))
    margin_ref[...] = margin_in[...] + row_sums(total * center - jnp.abs(total) * radius)


def product(scaled, weight, col, w_parts, final=None):
    specs, rows = scaled[0].shape
    group = len(scaled) // 2
    piece = w_parts[0][0].shape[-1]
    step = min(specs, 128)
    in_specs = [pl.BlockSpec((step, rows), lambda i, col: (i, 0)) for _ in scaled]
    in_specs.append(pl.BlockSpec((rows, piece), lambda i, col: (0, col[0])))
    args = [*scaled, weight]
    for array, place in w_parts:
        if array.ndim == 3:
            in_specs.append(pl.BlockSpec((None, rows, piece), lambda i, col, place=place: (place, 0, 0)))
        else:
            in_specs.append(pl.BlockSpec((rows, piece), lambda i, col: (0, 0)))
        args.append(array)
    block = pl.BlockSpec((step, piece), lambda i, col: (i, 0))
    kept = None
    aliases = {}
    if final is None:
        out_shape = jax.ShapeDtypeStruct((specs, piece), F32)
        out_specs = block
    else:
        sums, at, center, radius, margin, out = final
        near = center.shape[0]
        kept = (len(sums), near)
        in_specs += [block] * len(sums)
        box = pl.BlockSpec((near, piece), lambda i, col: (0, col[1]))
        line = pl.BlockSpec((8, step), lambda i, col: (0, i))
        in_specs += [pl.BlockSpec((step, at.shape[1]), lambda i, col: (i, 0)), box, box, line]
        args += [*sums, at, center, radius, margin]
        if out is not None:
            in_specs.append(pl.BlockSpec(memory_space=pl.ANY))
            args.append(out)
            aliases = {len(args): 0}
        out_shape = [jax.ShapeDtypeStruct((specs, QUARTERS * piece), F32), jax.ShapeDtypeStruct((8, specs), F32)]
        out_specs = [pl.BlockSpec((step, piece), lambda i, col: (i, col[1])), line]
    return pl.pallas_call(
        functools.partial(product_kernel, group, kept),
        out_shape=out_shape,
        grid_spec=pltpu.PrefetchScalarGridSpec(
            num_scalar_prefetch=1,
            grid=(specs // step,),
            in_specs=in_specs,
            out_specs=out_specs,
            scratch_shapes=[pltpu.VMEM((group * rows, piece), BF16)] * 2,
        ),
        input_output_aliases=aliases,
        compiler_params=pltpu.CompilerParams(vmem_limit_bytes=40 * 2**20),
        cost_estimate=pl.CostEstimate(
            flops=6 * specs * group * rows * piece, bytes_accessed=4 * group * rows * (specs + piece), transcendentals=0
        ),
    )(col, *args)


def local(members, sites, center, radius, weight, bias, out_weight, masks, image_labels, runner_up, spec_image):
    g, n = lax.axis_index("spec"), lax.axis_index("neuron")
    q = g % QUARTERS
    rows, cols = weight.shape[0], center.shape[1]
    images, specs, classes = center.shape[0], spec_image.shape[0], out_weight.shape[0]
    piece = cols // QUARTERS
    cut = sites // 2
    group = (0, 1, cut, cut + 1)
    far = [2 * m for m in range(1, sites // 4)]
    over_spec = functools.partial(swap, axis="spec", size=members)
    over_neuron = functools.partial(swap, axis="neuron", size=sites)

    boxes = jnp.stack([center, radius])[None]
    share = -(-classes // QUARTERS // 8) * 8

    def start_of(part):
        return jnp.minimum(part * share, classes - share)

    ow = {0: lax.dynamic_slice(out_weight, (start_of(q), 0), (share, rows))}
    ow[cut] = over_neuron(ow[0], k=cut)
    ow[1] = over_neuron(ow[0], k=1)
    ow[cut + 1] = over_neuron(ow[cut], k=1)

    order = [0]
    k = cut
    while k:
        boxes = jnp.concatenate([boxes, over_neuron(boxes, k=k)])
        order = order + [o ^ k for o in order]
        k //= 2
    spot = [order.index(o) for o in range(sites)]

    def columns(block):
        return lax.dynamic_slice(weight, (0, block * cols + q * piece), (rows, piece))

    targets = far + [0]
    home, last = {}, [boxes, ow[cut]]
    for t in targets:
        for j in (cut, cut + 1):
            send, last[0] = in_order(columns(n ^ j ^ t), last[0])
            home[t, j] = over_neuron(send, k=j)
            last = [last[1], home[t, j]]
    boxes, ow[cut] = boxes, ow[cut]
    beside = jnp.stack([columns(n ^ 1 ^ t) for t in targets])
    beside = over_neuron(beside, k=1)

    def spread(x):
        x2 = over_spec(x, k=2)
        return [x, over_spec(x, k=1), x2, over_spec(x2, k=1)]

    ow_parts = {j: spread(ow[j]) for j in group[1:]}
    beside_parts = spread(beside)
    w_parts = {key: spread(x) for key, x in home.items()}

    natural = jnp.zeros((sites,), jnp.int32)
    for o, s in enumerate(spot):
        natural = jnp.where((n ^ jnp.arange(sites)) == o, s, natural)
    full = jnp.take(boxes, natural, axis=0).transpose(1, 2, 0, 3).reshape(2, images, sites * cols)
    dims = (((1,), (1,)), ((), ()))
    pre_center = lax.dot_general(full[0], weight, dims, precision=lax.Precision.HIGH) + bias
    pre_radius = lax.dot_general(full[1], jnp.abs(weight), dims, precision=lax.Precision.HIGH)
    mask = lax.dynamic_slice(masks, (g * images, 0), (images, rows))
    upper, lower = pre_center + pre_radius, pre_center - pre_radius
    slope = jnp.clip(upper / (upper - lower), 0.0, 1.0)
    slopes = jnp.where(mask == 1, 1.0, jnp.where(mask == 2, slope, 0.0))
    offsets = jnp.where(mask == 2, slope * lower, 0.0)
    both = jnp.stack([slopes, offsets])
    near = jnp.stack([center, radius])
    k = 1
    while k < members:
        both = jnp.concatenate([both, over_spec(both, k=k)], axis=1)
        near = jnp.concatenate([near, over_spec(near, k=k)], axis=1)
        k *= 2
    slopes = {0: both[0]}
    slopes[cut] = over_neuron(slopes[0], k=cut)
    slopes[1] = over_neuron(slopes[0], k=1)
    slopes[cut + 1] = over_neuron(slopes[cut], k=1)

    labels = jnp.sum(jnp.where(spec_image[:, None] == jnp.arange(image_labels.shape[0]), image_labels, 0), axis=1)

    def place(label):
        part = label // share
        return (part ^ q) * share + label - start_of(part)

    at = jnp.stack(
        [
            place(labels),
            place(runner_up),
            ((spec_image // images) ^ g) * images + spec_image % images,
            labels,
            runner_up,
        ],
        axis=1,
    )
    *scaled, margin = scale(at, [out_weight], slopes[0], both[1], bias[None])
    for j in group[1:]:
        scaled += scale(at, ow_parts[j], slopes[j])

    out, sums = None, [[] for _ in range(QUARTERS)]
    for i, t in enumerate(targets):
        for r in range(QUARTERS):
            parts = [(beside_parts[r], i), (w_parts[t, cut][r], 0), (w_parts[t, cut + 1][r], 0)]
            col = jnp.stack([(n ^ t) * QUARTERS + (q ^ r), q ^ r])
            if t:
                sums[r].append(over_neuron(product(scaled, weight, col, parts), k=t))
            else:
                out, margin = product(
                    scaled, weight, col, parts, (sums[r], at, near[0], near[1], margin, out)
                )
    k = 1
    while k < sites:
        margin = margin + over_neuron(margin, k=k)
        k *= 2
    return out, margin[0]


def solution(mesh):
    members, sites = mesh.shape["spec"], mesh.shape["neuron"]
    return jax.shard_map(
        functools.partial(local, members, sites),
        mesh=mesh,
        in_specs=(
            P("spec", "neuron"),
            P("spec", "neuron"),
            P("neuron", None),
            P("neuron"),
            P(None, "neuron"),
            P(None, "neuron"),
            P(),
            P("spec"),
            P("spec"),
        ),
        out_specs=(P("spec", "neuron"), P("spec")),
        check_vma=False,
    )
```

```python
import functools

import jax
import jax.numpy as jnp
from jax import lax
from jax.experimental import pallas as pl
from jax.experimental.pallas import tpu as pltpu
from jax.sharding import PartitionSpec as P

QUARTERS = 4
F32, BF16 = jnp.float32, jnp.bfloat16
ROWS = (((1,), (0,)), ((), ()))
BOTH = (((1,), (1,)), ((), ()))
VMEM_BYTES = 40 * 2**20
MORE_VMEM_BYTES = 60 * 2**20


def swap(array, axis, size, k):
    return lax.ppermute(array, axis, [(i, i ^ k) for i in range(size)])


def dot(a, b, dims=ROWS):
    return lax.dot_general(a, b, dims, preferred_element_type=F32)


def two_terms(x):
    high = x.astype(BF16)
    return high, (x - high.astype(F32)).astype(BF16)


def three_terms(x):
    high = x.astype(BF16)
    rest = x - high.astype(F32)
    middle = rest.astype(BF16)
    return high, middle, (rest - middle.astype(F32)).astype(BF16)


def one_hot(index, size):
    return (index == lax.broadcasted_iota(jnp.int32, (index.shape[0], size), 1)).astype(F32)


def row_sums(x):
    ones = jnp.ones((8, x.shape[1]), BF16)
    return sum(dot(ones, term, BOTH) for term in three_terms(x))


def nothing():
    return pl.CostEstimate(flops=0, bytes_accessed=0, transcendentals=0)


def interval_kernel(spot_ref, boxes_ref, weight_ref, bias_ref, masks_ref, out_ref, center_sum, radius_sum):
    i = pl.program_id(0)
    images = boxes_ref.shape[1]
    weight = weight_ref[...]
    high, low = two_terms(weight)
    low_abs = jnp.where(weight < 0, -low.astype(F32), low.astype(F32)).astype(BF16)
    c = jnp.concatenate(two_terms(boxes_ref[0]), axis=0)
    r = jnp.concatenate(two_terms(boxes_ref[1]), axis=0)

    def both(x, y, box):
        main, rest = dot(x, box, BOTH), dot(y, box, BOTH)
        return main[:, :images] + (main[:, images:] + rest[:, :images])

    pre_center = both(high, low, c)
    pre_radius = both(jnp.abs(high), low_abs, r)

    @pl.when(i == 0)
    def _():
        center_sum[...] = pre_center
        radius_sum[...] = pre_radius

    @pl.when(i > 0)
    def _():
        center_sum[...] += pre_center
        radius_sum[...] += pre_radius

    @pl.when(i == pl.num_programs(0) - 1)
    def _():
        center, radius = center_sum[...].T + bias_ref[...], radius_sum[...].T
        upper, lower = center + radius, center - radius
        slope = jnp.clip(upper / (upper - lower), 0.0, 1.0)
        masks = masks_ref[...]
        out_ref[0] = jnp.where(masks == 1, 1.0, jnp.where(masks == 2, slope, 0.0))
        out_ref[1] = jnp.where(masks == 2, slope * lower, 0.0)


def interval(boxes, weight, bias, masks, spot):
    sites, _, images, cols = boxes.shape
    rows = weight.shape[0]
    return pl.pallas_call(
        interval_kernel,
        out_shape=jax.ShapeDtypeStruct((2, images, rows), F32),
        grid_spec=pltpu.PrefetchScalarGridSpec(
            num_scalar_prefetch=1,
            grid=(sites,),
            in_specs=[
                pl.BlockSpec((None, 2, images, cols), lambda i, spot: (spot[i], 0, 0, 0)),
                pl.BlockSpec((rows, cols), lambda i, spot: (0, i)),
                pl.BlockSpec((1, rows), lambda i, spot: (0, 0)),
                pl.BlockSpec((images, rows), lambda i, spot: (spot[sites], 0)),
            ],
            out_specs=pl.BlockSpec((2, images, rows), lambda i, spot: (0, 0, 0)),
            scratch_shapes=[pltpu.VMEM((rows, images), F32)] * 2,
        ),
        compiler_params=pltpu.CompilerParams(vmem_limit_bytes=VMEM_BYTES),
        cost_estimate=nothing(),
    )(spot, boxes, weight, bias, masks)


def scale_kernel(places, at_ref, slopes_ref, *refs):
    ow_refs, rest = refs[: len(places)], refs[len(places) :]
    at = at_ref[...]
    first = 0 if len(rest) == 1 else 3
    size = sum(shape[-2] for shape, _ in places)
    pick = (one_hot(at[:, first : first + 1], size) - one_hot(at[:, first + 1 : first + 2], size)).astype(BF16)
    coeff, low = None, 0
    for (shape, place), ref in zip(places, ow_refs):
        here = pick[:, low : low + shape[-2]]
        low += shape[-2]
        high_ow, low_ow = two_terms(ref[...] if place is None else ref[place])
        got = dot(here, high_ow) + dot(here, low_ow)
        coeff = got if coeff is None else coeff + got
    image = one_hot(at[:, 2:3], slopes_ref.shape[0]).astype(BF16)
    scaled = coeff * sum(dot(image, term) for term in three_terms(slopes_ref[...]))
    if first:
        offsets_ref, bias_ref, out_ref, relax_ref = rest
        offsets = sum(dot(image, term) for term in three_terms(offsets_ref[...]))
        relax_ref[...] = row_sums(scaled * bias_ref[...] - jnp.minimum(coeff, 0.0) * offsets)
    else:
        out_ref = rest[0]
    rows = scaled.shape[1]
    out_ref[:, :rows], out_ref[:, rows:] = two_terms(scaled)


def scale(at, ow_parts, slopes, *relax):
    specs, rows = at.shape[0], slopes.shape[1]
    outs = [jax.ShapeDtypeStruct((specs, 2 * rows), BF16)]
    if relax:
        outs = outs + [jax.ShapeDtypeStruct((8, specs), F32)]
    return pl.pallas_call(
        functools.partial(scale_kernel, [(array.shape, place) for array, place in ow_parts]),
        out_shape=outs,
        compiler_params=pltpu.CompilerParams(vmem_limit_bytes=VMEM_BYTES),
        cost_estimate=nothing(),
    )(at, slopes, *[array for array, _ in ow_parts], *relax)


def product_kernel(places, pieces, sums, *refs):
    group = len(places) // pieces
    col_ref, scaled_refs, weight_ref = refs[0], refs[1 : group + 2], refs[group + 2]
    w_refs, refs = refs[group + 3 : group + 3 + len(places)], refs[group + 3 + len(places) :]
    scaled_here, w_here, sems = refs[-3:]
    rows, piece = w_here.shape[1], w_here.shape[2] // pieces
    spans = [pl.ds(p * piece, piece) for p in range(pieces)]

    def columns(i):
        return pl.ds(pl.multiple_of(col_ref[i] * piece, piece), piece)

    sources = [weight_ref.at[:, columns(p)] for p in range(pieces)]
    sources += [ref if where is None else ref.at[where] for ref, where in zip(w_refs, places)]
    copies = []

    def fetch(source, target):
        copies.append(pltpu.make_async_copy(source, target, sems.at[len(copies)]))
        copies[-1].start()

    for j in range(group + 1):
        fetch(scaled_refs[j], scaled_here.at[j])
        for p in range(pieces):
            fetch(sources[j * pieces + p], w_here.at[j, :, spans[p]])
    operands = len(copies)
    if sums is not None:
        sum_refs, (near_ref, at_ref, margin_in) = refs[:sums], refs[sums : sums + 3]
        out_ref, margin_ref, block, near_here, sums_here = refs[-8:-3]
        for p in range(pieces):
            fetch(near_ref.at[:, :, columns(pieces + p)], near_here.at[:, :, spans[p]])
        for i, ref in enumerate(sum_refs):
            fetch(ref, sums_here.at[i])
    total = None
    for j in range(group + 1):
        for copy in copies[j * (pieces + 1) : (j + 1) * (pieces + 1)]:
            copy.wait()
        high, low = two_terms(w_here[j])
        got = dot(scaled_here[j], jnp.concatenate([high, high], axis=0)) + dot(scaled_here[j, :, :rows], low)
        total = got if total is None else total + got
    if sums is None:
        refs[0][...] = total
        return
    for copy in copies[operands:]:
        copy.wait()
    for i in range(sums):
        total = total + sums_here[i]
    block[...] = total
    puts = []
    for p in range(pieces):
        puts.append(pltpu.make_async_copy(block.at[:, spans[p]], out_ref.at[:, columns(pieces + p)], sems.at[p]))
        puts[-1].start()
    image = one_hot(at_ref[...][:, 5:6], near_here.shape[1]).astype(BF16)
    center = sum(dot(image, term) for term in three_terms(near_here[0]))
    radius = sum(dot(image, term) for term in three_terms(near_here[1]))
    margin_ref[...] = margin_in[...] + row_sums(total * center - jnp.abs(total) * radius)
    for put in puts:
        put.wait()


def product(scaled, weight, col, w_parts, final=None):
    specs, rows = scaled[0].shape[0], scaled[0].shape[1] // 2
    piece = w_parts[0][0].shape[-1]
    pieces = len(w_parts) // (len(scaled) - 1)
    whole = pl.BlockSpec(memory_space=pltpu.VMEM)
    there = pl.BlockSpec(memory_space=pltpu.HBM)
    args = [col, *scaled, weight, *[array for array, _ in w_parts]]
    in_specs = [pl.BlockSpec(memory_space=pltpu.SMEM)] + [there] * (len(args) - 1)
    scratch, n_sems = [], (1 + pieces) * len(scaled)
    aliases, sums = {}, None
    if final is None:
        out_shape, out_specs = jax.ShapeDtypeStruct((specs, pieces * piece), F32), whole
    else:
        sum_parts, at, near, margin, out = final
        sums = len(sum_parts)
        in_specs += [there] * (sums + 1) + [whole] * 2
        args += [*sum_parts, near, at, margin]
        if out is not None:
            aliases = {len(args): 0}
            in_specs.append(there)
            args.append(out)
        out_shape = [jax.ShapeDtypeStruct((specs, QUARTERS * piece), F32), jax.ShapeDtypeStruct((8, specs), F32)]
        out_specs = [there, whole]
        scratch = [
            pltpu.VMEM((specs, pieces * piece), F32),
            pltpu.VMEM((2, near.shape[1], pieces * piece), F32),
            pltpu.VMEM((sums, specs, pieces * piece), F32),
        ]
        n_sems += pieces + sums
    scratch += [
        pltpu.VMEM((len(scaled), specs, 2 * rows), BF16),
        pltpu.VMEM((len(scaled), rows, pieces * piece), F32),
        pltpu.SemaphoreType.DMA((n_sems,)),
    ]
    return pl.pallas_call(
        functools.partial(product_kernel, [place for _, place in w_parts], pieces, sums),
        out_shape=out_shape,
        in_specs=in_specs,
        out_specs=out_specs,
        scratch_shapes=scratch,
        input_output_aliases=aliases,
        compiler_params=pltpu.CompilerParams(vmem_limit_bytes=MORE_VMEM_BYTES),
        cost_estimate=nothing(),
    )(*args)


class Rounds:
    def __init__(self):
        self.got, self.fresh = {}, []

    def keep(self, name, value):
        self.got[name] = value
        self.fresh.append(name)

    def edge(self, *sends):
        held = [self.got[name] for name in self.fresh]
        done = lax.optimization_barrier((*[value for _, value, _ in sends], *held))
        self.got.update(zip(self.fresh, done[len(sends) :]))
        self.fresh = []
        for (name, _, move), value in zip(sends, done):
            self.keep(name, move(value))

    def send(self, name, value, move):
        self.keep(name, move(value))


def local(members, sites, center, radius, weight, bias, out_weight, masks, image_labels, runner_up, spec_image):
    g, n = lax.axis_index("spec"), lax.axis_index("neuron")
    q = g % QUARTERS
    rows, cols = weight.shape[0], center.shape[1]
    images, classes = center.shape[0], out_weight.shape[0]
    piece = cols // QUARTERS
    cut = sites // 2
    group = (1, cut, cut + 1)
    targets = [2 * m for m in range(1, sites // 4)] + [0]

    def to_site(k):
        return functools.partial(swap, axis="neuron", size=sites, k=k)

    def to_member(k):
        return functools.partial(swap, axis="spec", size=members, k=k)

    work = Rounds()
    got, keep, edge, send = work.got, work.keep, work.edge, work.send
    where = {}

    share = -(-classes // QUARTERS // 8) * 8

    def start_of(part):
        return jnp.minimum(part * share, classes - share)

    def columns(t, j):
        block = lax.dynamic_slice(weight, (0, (n ^ j ^ t) * cols + q * piece), (rows, piece))
        where[t, j, 0] = (t, j, 0), None
        return (t, j, 0), block, to_site(j)

    def part(name):
        key, place = where[name]
        return got[key], place

    def value(name):
        array, place = part(name)
        return array if place is None else array[place]

    def share_out(k, *names):
        pieces = [value(name) for name in names]
        names = [(what, j, r ^ k) for what, j, r in names]
        if len(names) == 1:
            where[names[0]] = names[0], None
            return names[0], pieces[0], to_member(k)
        for i, name in enumerate(names):
            where[name] = tuple(names), i
        return tuple(names), jnp.stack(pieces), to_member(k)

    ow = lax.dynamic_slice(out_weight, (start_of(q), 0), (share, rows))
    for j in group:
        where["ow", j, 0] = ("ow", j, 0), None
    send(("ow", 1, 0), ow, to_site(1))
    near = jnp.stack([center, radius])
    boxes = near[None]
    order = [0]
    k = cut
    while k:
        if k == 1:
            keep("boxes", boxes)
            edge((("ow", cut, 0), ow, to_site(cut)))
            boxes = got["boxes"]
        boxes = jnp.concatenate([boxes, to_site(k)(boxes)])
        order = order + [o ^ k for o in order]
        k //= 2
    keep("boxes", boxes)
    t = targets[0]
    send(*columns(t, 1))
    k = 1
    while k < members:
        near = jnp.concatenate([near, to_member(k)(near)], axis=1)
        k *= 2
    keep("near", near)
    spot = jnp.zeros((sites,), jnp.int32)
    for s, o in enumerate(order):
        spot = jnp.where((n ^ jnp.arange(sites)) == o, s, spot)

    edge(columns(t, cut))
    send(("ow", cut + 1, 0), got["ow", cut, 0], to_site(1))
    send(*share_out(2, ("ow", 1, 0)))
    send(*share_out(2, ("ow", cut, 0)))
    if len(targets) > 1:
        send(*columns(targets[1], 1))
    both = interval(got["boxes"], weight, bias[None], masks, jnp.append(spot, g))
    keep("both", lax.all_gather(both, "spec", axis=1, tiled=True))
    labels = jnp.sum(jnp.where(spec_image[:, None] == jnp.arange(image_labels.shape[0]), image_labels, 0), axis=1)

    def place(label):
        part = label // share
        return (part ^ q) * share + label - start_of(part)

    near_image = ((spec_image // images) ^ g) * images + spec_image % images
    keep("at", jnp.stack([place(labels), place(runner_up), spec_image, labels, runner_up, near_image], axis=1))

    edge(columns(t, cut + 1))
    send(*share_out(2, ("ow", cut + 1, 0)))
    send(*share_out(2, (t, 1, 0)))
    send(*share_out(1, *[("ow", j, r) for j in (1, cut) for r in (0, 2)]))
    slopes, offsets = got["both"][0], got["both"][1]
    keep("slopes", jnp.stack([slopes, to_site(cut)(slopes)]))
    *scaled, margin = scale(got["at"], [(out_weight, None)], slopes, offsets, bias[None])
    keep("scaled0", scaled[0])
    out, sums = None, {}

    def some_product(t, *members_at):
        parts = [part((t, j, r)) for j in group for r in members_at]
        col = jnp.stack([(n ^ t) * QUARTERS + (q ^ r) for r in members_at] + [q ^ r for r in members_at])
        scaled = [got["scaled0"]] + [got["scaled", j] for j in group]
        if t:
            return product(scaled, weight, col, parts)
        had = [got["sum", f, members_at] for f in targets[:-1]]
        return product(scaled, weight, col, parts, (had, got["at"], got["near"], margin, out))

    for i, t in enumerate(targets):
        after = targets[i + 1 :][:1]
        late = [cut, cut + 1] if i == 0 else [cut + 1]
        early = [j for j in group if j not in late]
        edge(*([columns(after[0], cut)] if after else []))
        if i:
            send(("sum", targets[i - 1], (2, 3)), got["product"], to_site(targets[i - 1]))
        if i == 0:
            slopes = jnp.concatenate([got["slopes"], to_site(1)(got["slopes"])])
        elif after:
            send(*columns(after[0], 1))
        send(*share_out(2, *[(t, j, 0) for j in late]))
        send(*share_out(1, *[(t, j, 0) for j in group], *[(t, j, 2) for j in early]))
        if i == 0:
            send(*share_out(1, ("ow", cut + 1, 0), ("ow", cut + 1, 2)))
            for j, slot in ((cut, 1), (1, 2), (cut + 1, 3)):
                parts = [part(("ow", j, r)) for r in range(QUARTERS)]
                (got["scaled", j],) = scale(got["at"], parts, slopes[slot])
        if t:
            keep("product", some_product(t, 0, 1))
        else:
            out, margin = some_product(t, 0, 1)
            keep("out", out)
            keep("margin", margin)
        edge(*([columns(after[0], cut + 1)] if after else []))
        if after:
            send(*share_out(2, (after[0], 1, 0), (after[0], cut, 0)))
        send(*share_out(1, *[(t, j, 2) for j in late]))
        if t:
            send(("sum", t, (0, 1)), got["product"], to_site(t))
            keep("product", some_product(t, 2, 3))
        else:
            out, margin = got["out"], got["margin"]
            out, margin = some_product(t, 2, 3)
    margin = margin + (to_site(1)(margin) + to_site(2)(margin) + to_site(3)(margin))
    k = 4
    while k < sites:
        margin = margin + to_site(k)(margin)
        k *= 2
    return out, margin[0]


def solution(mesh):
    members, sites = mesh.shape["spec"], mesh.shape["neuron"]
    return jax.shard_map(
        functools.partial(local, members, sites),
        mesh=mesh,
        in_specs=(
            P("spec", "neuron"),
            P("spec", "neuron"),
            P("neuron", None),
            P("neuron"),
            P(None, "neuron"),
            P(None, "neuron"),
            P(),
            P("spec"),
            P("spec"),
        ),
        out_specs=(P("spec", "neuron"), P("spec")),
        check_vma=False,
    )
```

```python
import functools

import jax
import jax.numpy as jnp
from jax import lax
from jax.experimental import pallas as pl
from jax.experimental.pallas import tpu as pltpu
from jax.sharding import PartitionSpec as P

QUARTERS = 4
F32, BF16 = jnp.float32, jnp.bfloat16
ROWS = (((1,), (0,)), ((), ()))
BOTH = (((1,), (1,)), ((), ()))
VMEM_BYTES = 40 * 2**20
MORE_VMEM_BYTES = 60 * 2**20


def swap(array, axis, size, k):
    return lax.ppermute(array, axis, [(i, i ^ k) for i in range(size)])


def dot(a, b, dims=ROWS):
    return lax.dot_general(a, b, dims, preferred_element_type=F32)


def two_terms(x):
    high = x.astype(BF16)
    return high, (x - high.astype(F32)).astype(BF16)


def three_terms(x):
    high = x.astype(BF16)
    rest = x - high.astype(F32)
    middle = rest.astype(BF16)
    return high, middle, (rest - middle.astype(F32)).astype(BF16)


def one_hot(index, size):
    return (index == lax.broadcasted_iota(jnp.int32, (index.shape[0], size), 1)).astype(F32)


def row_sums(x):
    ones = jnp.ones((8, x.shape[1]), BF16)
    return sum(dot(ones, term, BOTH) for term in three_terms(x))


def nothing():
    return pl.CostEstimate(flops=0, bytes_accessed=0, transcendentals=0)


def interval_kernel(spot_ref, boxes_ref, weight_ref, bias_ref, masks_ref, out_ref, center_sum, radius_sum):
    i = pl.program_id(0)
    images = boxes_ref.shape[1]
    weight = weight_ref[...]
    high, low = two_terms(weight)
    low_abs = jnp.where(weight < 0, -low.astype(F32), low.astype(F32)).astype(BF16)
    c = jnp.concatenate(two_terms(boxes_ref[0]), axis=0)
    r = jnp.concatenate(two_terms(boxes_ref[1]), axis=0)

    def both(x, y, box):
        main, rest = dot(x, box, BOTH), dot(y, box, BOTH)
        return main[:, :images] + (main[:, images:] + rest[:, :images])

    pre_center = both(high, low, c)
    pre_radius = both(jnp.abs(high), low_abs, r)

    @pl.when(i == 0)
    def _():
        center_sum[...] = pre_center
        radius_sum[...] = pre_radius

    @pl.when(i > 0)
    def _():
        center_sum[...] += pre_center
        radius_sum[...] += pre_radius

    @pl.when(i == pl.num_programs(0) - 1)
    def _():
        center, radius = center_sum[...].T + bias_ref[...], radius_sum[...].T
        upper, lower = center + radius, center - radius
        slope = jnp.clip(upper / (upper - lower), 0.0, 1.0)
        masks = masks_ref[...]
        out_ref[0] = jnp.where(masks == 1, 1.0, jnp.where(masks == 2, slope, 0.0))
        out_ref[1] = jnp.where(masks == 2, slope * lower, 0.0)


def interval(boxes, weight, bias, masks, spot):
    sites, _, images, cols = boxes.shape
    rows = weight.shape[0]
    return pl.pallas_call(
        interval_kernel,
        out_shape=jax.ShapeDtypeStruct((2, images, rows), F32),
        grid_spec=pltpu.PrefetchScalarGridSpec(
            num_scalar_prefetch=1,
            grid=(sites,),
            in_specs=[
                pl.BlockSpec((None, 2, images, cols), lambda i, spot: (spot[i], 0, 0, 0)),
                pl.BlockSpec((rows, cols), lambda i, spot: (0, i)),
                pl.BlockSpec((1, rows), lambda i, spot: (0, 0)),
                pl.BlockSpec((images, rows), lambda i, spot: (spot[sites], 0)),
            ],
            out_specs=pl.BlockSpec((2, images, rows), lambda i, spot: (0, 0, 0)),
            scratch_shapes=[pltpu.VMEM((rows, images), F32)] * 2,
        ),
        compiler_params=pltpu.CompilerParams(vmem_limit_bytes=VMEM_BYTES),
        cost_estimate=nothing(),
    )(spot, boxes, weight, bias, masks)


def scale_kernel(places, at_ref, slopes_ref, *refs):
    ow_refs, rest = refs[: len(places)], refs[len(places) :]
    at = at_ref[...]
    first = 0 if len(rest) == 1 else 3
    size = sum(shape[-2] for shape, _ in places)
    pick = (one_hot(at[:, first : first + 1], size) - one_hot(at[:, first + 1 : first + 2], size)).astype(BF16)
    coeff, low = None, 0
    for (shape, place), ref in zip(places, ow_refs):
        here = pick[:, low : low + shape[-2]]
        low += shape[-2]
        high_ow, low_ow = two_terms(ref[...] if place is None else ref[place])
        got = dot(here, high_ow) + dot(here, low_ow)
        coeff = got if coeff is None else coeff + got
    image = one_hot(at[:, 2:3], slopes_ref.shape[0]).astype(BF16)
    scaled = coeff * sum(dot(image, term) for term in three_terms(slopes_ref[...]))
    if first:
        offsets_ref, bias_ref, out_ref, relax_ref = rest
        offsets = sum(dot(image, term) for term in three_terms(offsets_ref[...]))
        relax_ref[...] = row_sums(scaled * bias_ref[...] - jnp.minimum(coeff, 0.0) * offsets)
    else:
        out_ref = rest[0]
    rows = scaled.shape[1]
    out_ref[:, :rows], out_ref[:, rows:] = two_terms(scaled)


def scale(at, ow_parts, slopes, *relax):
    specs, rows = at.shape[0], slopes.shape[1]
    outs = [jax.ShapeDtypeStruct((specs, 2 * rows), BF16)]
    if relax:
        outs = outs + [jax.ShapeDtypeStruct((8, specs), F32)]
    return pl.pallas_call(
        functools.partial(scale_kernel, [(array.shape, place) for array, place in ow_parts]),
        out_shape=outs,
        compiler_params=pltpu.CompilerParams(vmem_limit_bytes=VMEM_BYTES),
        cost_estimate=nothing(),
    )(at, slopes, *[array for array, _ in ow_parts], *relax)


def product_kernel(places, pieces, count, sum_places, *refs):
    col_ref, scaled_refs, refs = refs[0], refs[1 : count + 1], refs[count + 1 :]
    own_refs, refs = refs[: count * pieces - len(places)][:1], refs[min(1, count * pieces - len(places)) :]
    w_refs, refs = refs[: len(places)], refs[len(places) :]
    scaled_here, w_here, sems = refs[-3:]
    rows, piece = w_here.shape[1], w_here.shape[2] // pieces
    spans = [pl.ds(p * piece, piece) for p in range(pieces)]

    def columns(i):
        return pl.ds(pl.multiple_of(col_ref[i] * piece, piece), piece)

    sources = [ref.at[:, columns(p)] for ref in own_refs for p in range(pieces)]
    sources += [ref if where is None else ref.at[where] for ref, where in zip(w_refs, places)]
    copies = []

    def fetch(source, target):
        copies.append(pltpu.make_async_copy(source, target, sems.at[len(copies)]))
        copies[-1].start()

    for j in range(count):
        fetch(scaled_refs[j], scaled_here.at[j])
        for p in range(pieces):
            fetch(sources[j * pieces + p], w_here.at[j, :, spans[p]])
    operands = len(copies)
    if sum_places is not None:
        sums = len(sum_places)
        sum_refs, (near_ref, at_ref, margin_in) = refs[:sums], refs[sums : sums + 3]
        out_ref, margin_ref, block, near_here, sums_here = refs[-8:-3]
        for p in range(pieces):
            fetch(near_ref.at[:, :, columns(pieces + p)], near_here.at[:, :, spans[p]])
        for i, (ref, where) in enumerate(zip(sum_refs, sum_places)):
            (far, p, row), column = where
            target = sums_here.at[far, pl.ds(row, ref.shape[0]), spans[p]]
            fetch(ref.at[:, pl.ds(column * piece, piece)], target)
    total = None
    for j in range(count):
        for copy in copies[j * (pieces + 1) : (j + 1) * (pieces + 1)]:
            copy.wait()
        high, low = two_terms(w_here[j])
        got = dot(scaled_here[j], jnp.concatenate([high, high], axis=0)) + dot(scaled_here[j, :, :rows], low)
        total = got if total is None else total + got
    if sum_places is None:
        outs = refs[:-3]
        height = total.shape[0] // len(outs)
        for i, ref in enumerate(outs):
            ref[...] = total[i * height : (i + 1) * height]
        return
    for copy in copies[operands:]:
        copy.wait()
    for i in range(sums_here.shape[0]):
        total = total + sums_here[i]
    block[...] = total
    puts = []
    for p in range(pieces):
        puts.append(pltpu.make_async_copy(block.at[:, spans[p]], out_ref.at[:, columns(pieces + p)], sems.at[p]))
        puts[-1].start()
    image = one_hot(at_ref[...][:, 5:6], near_here.shape[1]).astype(BF16)
    center = sum(dot(image, term) for term in three_terms(near_here[0]))
    radius = sum(dot(image, term) for term in three_terms(near_here[1]))
    margin_ref[...] = margin_in[...] + row_sums(total * center - jnp.abs(total) * radius)
    for put in puts:
        put.wait()


def product(scaled, weight, col, w_parts, split=1, final=None):
    specs, rows = scaled[0].shape[0], scaled[0].shape[1] // 2
    piece = w_parts[0][0].shape[-1]
    pieces = col.shape[0] // 2
    weight = [weight] if len(w_parts) < len(scaled) * pieces else []
    whole = pl.BlockSpec(memory_space=pltpu.VMEM)
    there = pl.BlockSpec(memory_space=pltpu.HBM)
    args = [col, *scaled, *weight, *[array for array, _ in w_parts]]
    in_specs = [pl.BlockSpec(memory_space=pltpu.SMEM)] + [there] * (len(args) - 1)
    scratch, n_sems = [], (1 + pieces) * len(scaled)
    aliases, sum_places = {}, None
    if final is None:
        out_shape, out_specs = [jax.ShapeDtypeStruct((specs // split, pieces * piece), F32)] * split, [whole] * split
    else:
        sum_parts, at, near, margin, out = final
        sums, sum_places = len(sum_parts), [where for _, where in sum_parts]
        in_specs += [there] * (sums + 1) + [whole] * 2
        args += [*[array for array, _ in sum_parts], near, at, margin]
        if out is not None:
            aliases = {len(args): 0}
            in_specs.append(there)
            args.append(out)
        out_shape = [jax.ShapeDtypeStruct((specs, QUARTERS * piece), F32), jax.ShapeDtypeStruct((8, specs), F32)]
        out_specs = [there, whole]
        scratch = [
            pltpu.VMEM((specs, pieces * piece), F32),
            pltpu.VMEM((2, near.shape[1], pieces * piece), F32),
            pltpu.VMEM((1 + max(where[0][0] for where in sum_places), specs, pieces * piece), F32),
        ]
        n_sems += pieces + sums
    scratch += [
        pltpu.VMEM((len(scaled), specs, 2 * rows), BF16),
        pltpu.VMEM((len(scaled), rows, pieces * piece), F32),
        pltpu.SemaphoreType.DMA((n_sems,)),
    ]
    return pl.pallas_call(
        functools.partial(product_kernel, [place for _, place in w_parts], pieces, len(scaled), sum_places),
        out_shape=out_shape,
        in_specs=in_specs,
        out_specs=out_specs,
        scratch_shapes=scratch,
        input_output_aliases=aliases,
        compiler_params=pltpu.CompilerParams(vmem_limit_bytes=MORE_VMEM_BYTES),
        cost_estimate=nothing(),
    )(*args)


class Rounds:
    def __init__(self):
        self.got, self.fresh = {}, []

    def keep(self, name, value):
        self.got[name] = value
        self.fresh.append(name)

    def edge(self, *sends, only=None):
        names = self.fresh if only is None else only
        held = [self.got[name] for name in names]
        done = lax.optimization_barrier((*[value for _, value, _ in sends], *held))
        self.got.update(zip(names, done[len(sends) :]))
        self.fresh = [name for name in self.fresh if name not in names]
        for (name, _, move), value in zip(sends, done):
            self.keep(name, move(value))

    def send(self, name, value, move):
        self.keep(name, move(value))


def local(members, sites, center, radius, weight, bias, out_weight, masks, image_labels, runner_up, spec_image):
    g, n = lax.axis_index("spec"), lax.axis_index("neuron")
    q = g % QUARTERS
    rows, cols = weight.shape[0], center.shape[1]
    images, classes = center.shape[0], out_weight.shape[0]
    piece = cols // QUARTERS
    cut = sites // 2
    pair = 2
    group = (pair, cut, cut + pair)
    targets = [m for m in range(1, sites) if not m & (cut + pair)] + [0]

    def to_site(k):
        return functools.partial(swap, axis="neuron", size=sites, k=k)

    def to_member(k):
        return functools.partial(swap, axis="spec", size=members, k=k)

    work = Rounds()
    got, keep, edge, send = work.got, work.keep, work.edge, work.send
    where = {}

    share = -(-classes // QUARTERS // 8) * 8

    def start_of(part):
        return jnp.minimum(part * share, classes - share)

    def columns(t, j):
        block = lax.dynamic_slice(weight, (0, (n ^ j ^ t) * cols + q * piece), (rows, piece))
        where[t, j, 0] = (t, j, 0), None
        return (t, j, 0), block, to_site(j)

    def part(name):
        key, place = where[name]
        return got[key], place

    def value(name):
        array, place = part(name)
        return array if place is None else array[place]

    def share_out(k, *names):
        pieces = [value(name) for name in names]
        names = [(what, j, r ^ k) for what, j, r in names]
        if len(names) == 1:
            where[names[0]] = names[0], None
            return names[0], pieces[0], to_member(k)
        for i, name in enumerate(names):
            where[name] = tuple(names), i
        return tuple(names), jnp.stack(pieces), to_member(k)

    ow = lax.dynamic_slice(out_weight, (start_of(q), 0), (share, rows))
    for j in group:
        where["ow", j, 0] = ("ow", j, 0), None
    t = targets[0]
    near = jnp.stack([center, radius])
    boxes = near[None]
    order = [0]
    k = cut
    while k:
        if k == 1:
            keep("boxes", boxes)
            edge((("ow", cut, 0), ow, to_site(cut)), (("ow", pair, 0), ow, to_site(pair)), only=["boxes"])
            boxes = got["boxes"]
        boxes = jnp.concatenate([boxes, to_site(k)(boxes)])
        order = order + [o ^ k for o in order]
        k //= 2
    keep("boxes", boxes)
    k = 1
    while k < members:
        near = jnp.concatenate([near, to_member(k)(near)], axis=1)
        k *= 2
    keep("near", near)
    spot = jnp.zeros((sites,), jnp.int32)
    for s, o in enumerate(order):
        spot = jnp.where((n ^ jnp.arange(sites)) == o, s, spot)

    edge(columns(t, cut))
    send(("ow", cut + pair, 0), got["ow", cut, 0], to_site(pair))
    send(*share_out(2, ("ow", pair, 0)))
    send(*share_out(2, ("ow", cut, 0)))
    both = interval(got["boxes"], weight, bias[None], masks, jnp.append(spot, g))
    keep("both", lax.all_gather(both, "spec", axis=1, tiled=True))
    labels = jnp.sum(jnp.where(spec_image[:, None] == jnp.arange(image_labels.shape[0]), image_labels, 0), axis=1)

    def place(label):
        part = label // share
        return (part ^ q) * share + label - start_of(part)

    near_image = ((spec_image // images) ^ g) * images + spec_image % images
    keep("at", jnp.stack([place(labels), place(runner_up), spec_image, labels, runner_up, near_image], axis=1))

    edge(columns(t, cut + pair), columns(t, pair))
    send(*share_out(2, ("ow", cut + pair, 0)))
    send(*share_out(2, (t, cut, 0)))
    slopes, offsets = got["both"][0], got["both"][1]
    slopes = jnp.stack([slopes, to_site(pair)(slopes)])
    slopes = jnp.concatenate([slopes, to_site(cut)(slopes)])
    keep("slopes", slopes)
    slopes = slopes[0]
    scaled, margin = scale(got["at"], [(out_weight, None)], slopes, offsets, bias[None])
    keep("margin", margin)
    keep(("scaled", 0), scaled)

    sum_parts = {}

    def some_product(t, *members_at, sites=(0, *group), last=True):
        parts = [part((t, j, r)) for j in sites if j for r in members_at]
        col = jnp.stack([(n ^ t) * QUARTERS + (q ^ r) for r in members_at] + [q ^ r for r in members_at])
        scaled = [got["scaled", j] for j in sites]
        if t or not last:
            (made,) = product(scaled, weight, col, parts)
            keep(("product", t, members_at), made)
            return
        had = []
        for i, f in enumerate(targets):
            for p, r in enumerate(members_at):
                if f:
                    had.append((got["sum", f, members_at], ((i, p, 0), p)))
                elif len(sites) <= len(group):
                    had.append((got["product", t, members_at], ((i, p, 0), p)))
        final = had, got["at"], got["near"], got["margin"], got.get("out")
        out, margin = product(scaled, weight, col, parts, final=final)
        keep("out", out)
        keep("margin", margin)

    def send_sum(t, *members_at):
        send(("sum", t, members_at), got["product", t, members_at], to_site(t))

    for i, t in enumerate(targets):
        after = targets[i + 1 :][:1]
        edge(*([columns(after[0], cut), columns(after[0], pair)] if after else []))
        if i:
            send_sum(targets[i - 1], 2, 3)
        else:
            slopes = got["slopes"]
        if i == 0:
            send(*share_out(2, (t, pair, 0)))
        send(*share_out(2, (t, cut + pair, 0)))
        if t:
            send(*share_out(1, *[(t, j, 0) for j in group]))
        else:
            send(*share_out(1, (t, pair, 0), (t, cut, 0)))
            send(*share_out(1, (t, cut + pair, 0)))
            send(*share_out(1, (t, pair, 2), (t, cut, 2)))
        if i == 0:
            send(*share_out(1, *[("ow", j, r) for j in group for r in (0, 2)]))
            for j, slot in ((pair, 1), (cut, 2), (cut + pair, 3)):
                parts = [part(("ow", j, r)) for r in range(QUARTERS)]
                (got["scaled", j],) = scale(got["at"], parts, slopes[slot])
        some_product(t, 0, 1)
        if not t:
            some_product(t, 2, 3, sites=(0, pair, cut), last=False)
        names = [name for name in work.fresh if name[0] != "sum" or t]
        edge(*([columns(after[0], cut + pair)] if after else []), only=names)
        if after:
            send(*share_out(2, (after[0], cut, 0)))
            send(*share_out(2, (after[0], pair, 0)))
        if t:
            send(*share_out(1, *[(t, j, 2) for j in group]))
            send_sum(t, 0, 1)
            some_product(t, 2, 3)
        else:
            send(*share_out(1, (t, cut + pair, 2)))
            some_product(t, 2, 3, sites=(cut + pair,))
    out, margin = got["out"], got["margin"]
    margin = margin + (to_site(1)(margin) + to_site(2)(margin) + to_site(3)(margin))
    k = 4
    while k < sites:
        margin = margin + to_site(k)(margin)
        k *= 2
    return out, margin[0]


def solution(mesh):
    members, sites = mesh.shape["spec"], mesh.shape["neuron"]
    return jax.shard_map(
        functools.partial(local, members, sites),
        mesh=mesh,
        in_specs=(
            P("spec", "neuron"),
            P("spec", "neuron"),
            P("neuron", None),
            P("neuron"),
            P(None, "neuron"),
            P(None, "neuron"),
            P(),
            P("spec"),
            P("spec"),
        ),
        out_specs=(P("spec", "neuron"), P("spec")),
        check_vma=False,
    )
```

```python
import functools

import jax
import jax.numpy as jnp
from jax import lax
from jax.experimental import pallas as pl
from jax.experimental.pallas import tpu as pltpu
from jax.sharding import PartitionSpec as P

QUARTERS = 4
F32, BF16 = jnp.float32, jnp.bfloat16
ROWS = (((1,), (0,)), ((), ()))
BOTH = (((1,), (1,)), ((), ()))
VMEM_BYTES = 40 * 2**20
MORE_VMEM_BYTES = 60 * 2**20


def swap(array, axis, size, k):
    return lax.ppermute(array, axis, [(i, i ^ k) for i in range(size)])


def dot(a, b, dims=ROWS):
    return lax.dot_general(a, b, dims, preferred_element_type=F32)


def two_terms(x):
    high = x.astype(BF16)
    return high, (x - high.astype(F32)).astype(BF16)


def three_terms(x):
    high = x.astype(BF16)
    rest = x - high.astype(F32)
    middle = rest.astype(BF16)
    return high, middle, (rest - middle.astype(F32)).astype(BF16)


def one_hot(index, size):
    return (index == lax.broadcasted_iota(jnp.int32, (index.shape[0], size), 1)).astype(F32)


def row_sums(x):
    ones = jnp.ones((8, x.shape[1]), BF16)
    return sum(dot(ones, term, BOTH) for term in three_terms(x))


def nothing():
    return pl.CostEstimate(flops=0, bytes_accessed=0, transcendentals=0)


def interval_kernel(spot_ref, boxes_ref, weight_ref, bias_ref, masks_ref, out_ref, center_sum, radius_sum):
    i = pl.program_id(0)
    images = boxes_ref.shape[1]
    weight = weight_ref[...]
    high, low = two_terms(weight)
    low_abs = jnp.where(weight < 0, -low.astype(F32), low.astype(F32)).astype(BF16)
    c = jnp.concatenate(two_terms(boxes_ref[0]), axis=0)
    r = jnp.concatenate(two_terms(boxes_ref[1]), axis=0)

    def both(x, y, box):
        main, rest = dot(x, box, BOTH), dot(y, box, BOTH)
        return main[:, :images] + (main[:, images:] + rest[:, :images])

    pre_center = both(high, low, c)
    pre_radius = both(jnp.abs(high), low_abs, r)

    @pl.when(i == 0)
    def _():
        center_sum[...] = pre_center
        radius_sum[...] = pre_radius

    @pl.when(i > 0)
    def _():
        center_sum[...] += pre_center
        radius_sum[...] += pre_radius

    @pl.when(i == pl.num_programs(0) - 1)
    def _():
        center, radius = center_sum[...].T + bias_ref[...], radius_sum[...].T
        upper, lower = center + radius, center - radius
        slope = jnp.clip(upper / (upper - lower), 0.0, 1.0)
        masks = masks_ref[...]
        out_ref[0] = jnp.where(masks == 1, 1.0, jnp.where(masks == 2, slope, 0.0))
        out_ref[1] = jnp.where(masks == 2, slope * lower, 0.0)


def interval(boxes, weight, bias, masks, spot):
    sites, _, images, cols = boxes.shape
    rows = weight.shape[0]
    return pl.pallas_call(
        interval_kernel,
        out_shape=jax.ShapeDtypeStruct((2, images, rows), F32),
        grid_spec=pltpu.PrefetchScalarGridSpec(
            num_scalar_prefetch=1,
            grid=(sites,),
            in_specs=[
                pl.BlockSpec((None, 2, images, cols), lambda i, spot: (spot[i], 0, 0, 0)),
                pl.BlockSpec((rows, cols), lambda i, spot: (0, i)),
                pl.BlockSpec((1, rows), lambda i, spot: (0, 0)),
                pl.BlockSpec((images, rows), lambda i, spot: (spot[sites], 0)),
            ],
            out_specs=pl.BlockSpec((2, images, rows), lambda i, spot: (0, 0, 0)),
            scratch_shapes=[pltpu.VMEM((rows, images), F32)] * 2,
        ),
        compiler_params=pltpu.CompilerParams(vmem_limit_bytes=VMEM_BYTES),
        cost_estimate=nothing(),
    )(spot, boxes, weight, bias, masks)


def scale_kernel(places, at_ref, slopes_ref, *refs):
    ow_refs, rest = refs[: len(places)], refs[len(places) :]
    at = at_ref[...]
    first = 0 if len(rest) == 1 else 3
    size = sum(shape[-2] for shape, _ in places)
    pick = (one_hot(at[:, first : first + 1], size) - one_hot(at[:, first + 1 : first + 2], size)).astype(BF16)
    coeff, low = None, 0
    for (shape, place), ref in zip(places, ow_refs):
        here = pick[:, low : low + shape[-2]]
        low += shape[-2]
        high_ow, low_ow = two_terms(ref[...] if place is None else ref[place])
        got = dot(here, high_ow) + dot(here, low_ow)
        coeff = got if coeff is None else coeff + got
    image = one_hot(at[:, 2:3], slopes_ref.shape[0]).astype(BF16)
    scaled = coeff * sum(dot(image, term) for term in three_terms(slopes_ref[...]))
    if first:
        offsets_ref, bias_ref, out_ref, relax_ref = rest
        offsets = sum(dot(image, term) for term in three_terms(offsets_ref[...]))
        relax_ref[...] = row_sums(scaled * bias_ref[...] - jnp.minimum(coeff, 0.0) * offsets)
    else:
        out_ref = rest[0]
    rows = scaled.shape[1]
    out_ref[:, :rows], out_ref[:, rows:] = two_terms(scaled)


def scale(at, ow_parts, slopes, *relax):
    specs, rows = at.shape[0], slopes.shape[1]
    outs = [jax.ShapeDtypeStruct((specs, 2 * rows), BF16)]
    if relax:
        outs = outs + [jax.ShapeDtypeStruct((8, specs), F32)]
    return pl.pallas_call(
        functools.partial(scale_kernel, [(array.shape, place) for array, place in ow_parts]),
        out_shape=outs,
        compiler_params=pltpu.CompilerParams(vmem_limit_bytes=VMEM_BYTES),
        cost_estimate=nothing(),
    )(at, slopes, *[array for array, _ in ow_parts], *relax)


def product_kernel(places, pieces, count, sum_places, *refs):
    col_ref, scaled_refs, refs = refs[0], refs[1 : count + 1], refs[count + 1 :]
    own_refs, refs = refs[: count * pieces - len(places)][:1], refs[min(1, count * pieces - len(places)) :]
    w_refs, refs = refs[: len(places)], refs[len(places) :]
    scaled_here, w_here, sems = refs[-3:]
    rows, piece = w_here.shape[1], w_here.shape[2] // pieces
    spans = [pl.ds(p * piece, piece) for p in range(pieces)]

    def columns(i):
        return pl.ds(pl.multiple_of(col_ref[i] * piece, piece), piece)

    sources = [ref.at[:, columns(p)] for ref in own_refs for p in range(pieces)]
    sources += [ref if where is None else ref.at[where] for ref, where in zip(w_refs, places)]
    copies = []

    def fetch(source, target):
        copies.append(pltpu.make_async_copy(source, target, sems.at[len(copies)]))
        copies[-1].start()

    for j in range(count):
        fetch(scaled_refs[j], scaled_here.at[j])
        for p in range(pieces):
            fetch(sources[j * pieces + p], w_here.at[j, :, spans[p]])
    operands = len(copies)
    if sum_places is not None:
        sums = len(sum_places)
        sum_refs, (near_ref, at_ref, margin_in) = refs[:sums], refs[sums : sums + 3]
        out_ref, margin_ref, block, near_here, sums_here = refs[-8:-3]
        for p in range(pieces):
            fetch(near_ref.at[:, :, columns(pieces + p)], near_here.at[:, :, spans[p]])
        for i, (ref, where) in enumerate(zip(sum_refs, sum_places)):
            (far, p, row), column = where
            target = sums_here.at[far, pl.ds(row, ref.shape[0]), spans[p]]
            fetch(ref.at[:, pl.ds(column * piece, piece)], target)
    total = None
    for j in range(count):
        for copy in copies[j * (pieces + 1) : (j + 1) * (pieces + 1)]:
            copy.wait()
        high, low = two_terms(w_here[j])
        got = dot(scaled_here[j], jnp.concatenate([high, high], axis=0)) + dot(scaled_here[j, :, :rows], low)
        total = got if total is None else total + got
    if sum_places is None:
        outs = refs[:-3]
        height = total.shape[0] // len(outs)
        for i, ref in enumerate(outs):
            ref[...] = total[i * height : (i + 1) * height]
        return
    for copy in copies[operands:]:
        copy.wait()
    for i in range(sums_here.shape[0]):
        total = total + sums_here[i]
    block[...] = total
    puts = []
    for p in range(pieces):
        puts.append(pltpu.make_async_copy(block.at[:, spans[p]], out_ref.at[:, columns(pieces + p)], sems.at[p]))
        puts[-1].start()
    image = one_hot(at_ref[...][:, 5:6], near_here.shape[1]).astype(BF16)
    center = sum(dot(image, term) for term in three_terms(near_here[0]))
    radius = sum(dot(image, term) for term in three_terms(near_here[1]))
    margin_ref[...] = margin_in[...] + row_sums(total * center - jnp.abs(total) * radius)
    for put in puts:
        put.wait()


def product(scaled, weight, col, w_parts, split=1, final=None):
    specs, rows = scaled[0].shape[0], scaled[0].shape[1] // 2
    piece = w_parts[0][0].shape[-1]
    pieces = col.shape[0] // 2
    weight = [weight] if len(w_parts) < len(scaled) * pieces else []
    whole = pl.BlockSpec(memory_space=pltpu.VMEM)
    there = pl.BlockSpec(memory_space=pl.ANY if len(scaled) == 1 else pltpu.HBM)
    args = [col, *scaled, *weight, *[array for array, _ in w_parts]]
    in_specs = [pl.BlockSpec(memory_space=pltpu.SMEM)] + [there] * (len(args) - 1)
    scratch, n_sems = [], (1 + pieces) * len(scaled)
    aliases, sum_places = {}, None
    if final is None:
        out_shape, out_specs = [jax.ShapeDtypeStruct((specs // split, pieces * piece), F32)] * split, [whole] * split
    else:
        sum_parts, at, near, margin, out = final
        sums, sum_places = len(sum_parts), [where for _, where in sum_parts]
        in_specs += [there] * (sums + 1) + [whole] * 2
        args += [*[array for array, _ in sum_parts], near, at, margin]
        if out is not None:
            aliases = {len(args): 0}
            in_specs.append(there)
            args.append(out)
        out_shape = [jax.ShapeDtypeStruct((specs, QUARTERS * piece), F32), jax.ShapeDtypeStruct((8, specs), F32)]
        out_specs = [there, whole]
        scratch = [
            pltpu.VMEM((specs, pieces * piece), F32),
            pltpu.VMEM((2, near.shape[1], pieces * piece), F32),
            pltpu.VMEM((1 + max(where[0][0] for where in sum_places), specs, pieces * piece), F32),
        ]
        n_sems += pieces + sums
    scratch += [
        pltpu.VMEM((len(scaled), specs, 2 * rows), BF16),
        pltpu.VMEM((len(scaled), rows, pieces * piece), F32),
        pltpu.SemaphoreType.DMA((n_sems,)),
    ]
    return pl.pallas_call(
        functools.partial(product_kernel, [place for _, place in w_parts], pieces, len(scaled), sum_places),
        out_shape=out_shape,
        in_specs=in_specs,
        out_specs=out_specs,
        scratch_shapes=scratch,
        input_output_aliases=aliases,
        compiler_params=pltpu.CompilerParams(vmem_limit_bytes=MORE_VMEM_BYTES if weight else VMEM_BYTES),
        cost_estimate=nothing(),
    )(*args)


class Rounds:
    def __init__(self):
        self.got, self.fresh = {}, []

    def keep(self, name, value):
        self.got[name] = value
        self.fresh.append(name)

    def edge(self, *sends, only=None):
        names = self.fresh if only is None else only
        held = [self.got[name] for name in names]
        done = lax.optimization_barrier((*[value for _, value, _ in sends], *held))
        self.got.update(zip(names, done[len(sends) :]))
        self.fresh = [name for name in self.fresh if name not in names]
        for (name, _, move), value in zip(sends, done):
            self.keep(name, move(value))

    def send(self, name, value, move):
        self.keep(name, move(value))


def local(members, sites, center, radius, weight, bias, out_weight, masks, image_labels, runner_up, spec_image):
    g, n = lax.axis_index("spec"), lax.axis_index("neuron")
    q = g % QUARTERS
    rows, cols = weight.shape[0], center.shape[1]
    images, classes = center.shape[0], out_weight.shape[0]
    piece = cols // QUARTERS
    cut = sites // 2
    pair = 2
    group = (pair, cut, cut + pair)
    targets = [m for m in range(1, sites) if not m & (cut + pair)] + [0]

    def to_site(k):
        return functools.partial(swap, axis="neuron", size=sites, k=k)

    def to_member(k):
        return functools.partial(swap, axis="spec", size=members, k=k)

    work = Rounds()
    got, keep, edge, send = work.got, work.keep, work.edge, work.send
    where = {}

    share = -(-classes // QUARTERS // 8) * 8

    def start_of(part):
        return jnp.minimum(part * share, classes - share)

    def columns(t, j):
        block = lax.dynamic_slice(weight, (0, (n ^ j ^ t) * cols + q * piece), (rows, piece))
        where[t, j, 0] = (t, j, 0), None
        return (t, j, 0), block, to_site(j)

    def part(name):
        key, place = where[name]
        return got[key], place

    def value(name):
        array, place = part(name)
        return array if place is None else array[place]

    def share_out(k, *names):
        pieces = [value(name) for name in names]
        names = [(what, j, r ^ k) for what, j, r in names]
        if len(names) == 1:
            where[names[0]] = names[0], None
            return names[0], pieces[0], to_member(k)
        for i, name in enumerate(names):
            where[name] = tuple(names), i
        return tuple(names), jnp.stack(pieces), to_member(k)

    ow = lax.dynamic_slice(out_weight, (start_of(q), 0), (share, rows))
    for j in group:
        where["ow", j, 0] = ("ow", j, 0), None
    t = targets[0]
    near = jnp.stack([center, radius])
    boxes = near[None]
    order = [0]
    k = cut
    while k:
        if k == 1:
            keep("boxes", boxes)
            edge((("ow", cut, 0), ow, to_site(cut)), (("ow", pair, 0), ow, to_site(pair)), only=["boxes"])
            boxes = got["boxes"]
        boxes = jnp.concatenate([boxes, to_site(k)(boxes)])
        order = order + [o ^ k for o in order]
        k //= 2
    keep("boxes", boxes)
    k = 1
    while k < members:
        near = jnp.concatenate([near, to_member(k)(near)], axis=1)
        k *= 2
    keep("near", near)
    spot = jnp.zeros((sites,), jnp.int32)
    for s, o in enumerate(order):
        spot = jnp.where((n ^ jnp.arange(sites)) == o, s, spot)

    edge(columns(t, cut))
    send(("ow", cut + pair, 0), got["ow", cut, 0], to_site(pair))
    send(*share_out(2, ("ow", pair, 0)))
    send(*share_out(2, ("ow", cut, 0)))
    both = interval(got["boxes"], weight, bias[None], masks, jnp.append(spot, g))
    keep("both", lax.all_gather(both, "spec", axis=1, tiled=True))
    labels = jnp.sum(jnp.where(spec_image[:, None] == jnp.arange(image_labels.shape[0]), image_labels, 0), axis=1)

    def place(label):
        part = label // share
        return (part ^ q) * share + label - start_of(part)

    near_image = ((spec_image // images) ^ g) * images + spec_image % images
    keep("at", jnp.stack([place(labels), place(runner_up), spec_image, labels, runner_up, near_image], axis=1))

    edge(columns(t, cut + pair), columns(t, pair))
    send(*share_out(2, ("ow", cut + pair, 0)))
    send(*share_out(2, (t, cut, 0)))
    slopes, offsets = got["both"][0], got["both"][1]
    slopes = jnp.stack([slopes, to_site(pair)(slopes)])
    slopes = jnp.concatenate([slopes, to_site(cut)(slopes)])
    keep("slopes", slopes)
    slopes = slopes[0]
    scaled, margin = scale(got["at"], [(out_weight, None)], slopes, offsets, bias[None])
    keep("margin", margin)
    keep(("scaled", 0), scaled)

    sum_parts = {}

    def some_product(t, *members_at, sites=(0, *group), last=True):
        parts = [part((t, j, r)) for j in sites if j for r in members_at]
        col = jnp.stack([(n ^ t) * QUARTERS + (q ^ r) for r in members_at] + [q ^ r for r in members_at])
        scaled = [got["scaled", j] for j in sites]
        if t or not last:
            (made,) = product(scaled, weight, col, parts)
            keep(("product", t, members_at), made)
            return
        had = []
        for i, f in enumerate(targets):
            for p, r in enumerate(members_at):
                if f:
                    had.append((got["sum", f, members_at], ((i, p, 0), p)))
                elif len(sites) <= len(group):
                    had.append((got["product", t, members_at], ((i, p, 0), p)))
        final = had, got["at"], got["near"], got["margin"], got.get("out")
        out, margin = product(scaled, weight, col, parts, final=final)
        keep("out", out)
        keep("margin", margin)

    def send_sum(t, *members_at):
        send(("sum", t, members_at), got["product", t, members_at], to_site(t))

    for i, t in enumerate(targets):
        after = targets[i + 1 :][:1]
        edge(*([columns(after[0], cut), columns(after[0], pair)] if after else []))
        if i:
            send_sum(targets[i - 1], 2, 3)
        else:
            slopes = got["slopes"]
        if i == 0:
            send(*share_out(2, (t, pair, 0)))
        send(*share_out(2, (t, cut + pair, 0)))
        if t:
            send(*share_out(1, *[(t, j, 0) for j in group]))
        else:
            send(*share_out(1, (t, pair, 0), (t, cut, 0)))
            send(*share_out(1, (t, cut + pair, 0)))
            send(*share_out(1, (t, pair, 2), (t, cut, 2)))
        if i == 0:
            send(*share_out(1, *[("ow", j, r) for j in group for r in (0, 2)]))
            for j, slot in ((pair, 1), (cut, 2), (cut + pair, 3)):
                parts = [part(("ow", j, r)) for r in range(QUARTERS)]
                (got["scaled", j],) = scale(got["at"], parts, slopes[slot])
        some_product(t, 0, 1)
        if not t:
            some_product(t, 2, 3, sites=(0, pair, cut), last=False)
        names = [name for name in work.fresh if name[0] != "sum" or t]
        edge(*([columns(after[0], cut + pair)] if after else []), only=names)
        if after:
            send(*share_out(2, (after[0], cut, 0)))
            send(*share_out(2, (after[0], pair, 0)))
        if t:
            send(*share_out(1, *[(t, j, 2) for j in group]))
            send_sum(t, 0, 1)
            some_product(t, 2, 3)
        else:
            send(*share_out(1, (t, cut + pair, 2)))
            some_product(t, 2, 3, sites=(cut + pair,))
    out, margin = got["out"], got["margin"]
    margin = margin + (to_site(1)(margin) + to_site(2)(margin) + to_site(3)(margin))
    k = 4
    while k < sites:
        margin = margin + to_site(k)(margin)
        k *= 2
    return out, margin[0]


def solution(mesh):
    members, sites = mesh.shape["spec"], mesh.shape["neuron"]
    return jax.shard_map(
        functools.partial(local, members, sites),
        mesh=mesh,
        in_specs=(
            P("spec", "neuron"),
            P("spec", "neuron"),
            P("neuron", None),
            P("neuron"),
            P(None, "neuron"),
            P(None, "neuron"),
            P(),
            P("spec"),
            P("spec"),
        ),
        out_specs=(P("spec", "neuron"), P("spec")),
        check_vma=False,
    )
```

```python
import functools

import jax
import jax.numpy as jnp
from jax import lax
from jax.experimental import pallas as pl
from jax.experimental.pallas import tpu as pltpu
from jax.sharding import PartitionSpec as P

QUARTERS = 4
F32, BF16 = jnp.float32, jnp.bfloat16
ROWS = (((1,), (0,)), ((), ()))
BOTH = (((1,), (1,)), ((), ()))
VMEM_BYTES = 40 * 2**20
MORE_VMEM_BYTES = 60 * 2**20


def swap(array, axis, size, k):
    return lax.ppermute(array, axis, [(i, i ^ k) for i in range(size)])


def dot(a, b, dims=ROWS):
    return lax.dot_general(a, b, dims, preferred_element_type=F32)


def two_terms(x):
    high = x.astype(BF16)
    return high, (x - high.astype(F32)).astype(BF16)


def three_terms(x):
    high = x.astype(BF16)
    rest = x - high.astype(F32)
    middle = rest.astype(BF16)
    return high, middle, (rest - middle.astype(F32)).astype(BF16)


def one_hot(index, size):
    return (index == lax.broadcasted_iota(jnp.int32, (index.shape[0], size), 1)).astype(F32)


def row_sums(x):
    ones = jnp.ones((8, x.shape[1]), BF16)
    return sum(dot(ones, term, BOTH) for term in three_terms(x))


def nothing():
    return pl.CostEstimate(flops=0, bytes_accessed=0, transcendentals=0)


def interval_kernel(spot_ref, boxes_ref, weight_ref, bias_ref, masks_ref, out_ref, center_sum, radius_sum):
    i = pl.program_id(0)
    images = boxes_ref.shape[1]
    weight = weight_ref[...]
    high, low = two_terms(weight)
    low_abs = jnp.where(weight < 0, -low.astype(F32), low.astype(F32)).astype(BF16)
    c = jnp.concatenate(two_terms(boxes_ref[0]), axis=0)
    r = jnp.concatenate(two_terms(boxes_ref[1]), axis=0)

    def both(x, y, box):
        main, rest = dot(x, box, BOTH), dot(y, box, BOTH)
        return main[:, :images] + (main[:, images:] + rest[:, :images])

    pre_center = both(high, low, c)
    pre_radius = both(jnp.abs(high), low_abs, r)

    @pl.when(i == 0)
    def _():
        center_sum[...] = pre_center
        radius_sum[...] = pre_radius

    @pl.when(i > 0)
    def _():
        center_sum[...] += pre_center
        radius_sum[...] += pre_radius

    @pl.when(i == pl.num_programs(0) - 1)
    def _():
        center, radius = center_sum[...].T + bias_ref[...], radius_sum[...].T
        upper, lower = center + radius, center - radius
        slope = jnp.clip(upper / (upper - lower), 0.0, 1.0)
        masks = masks_ref[...]
        out_ref[0] = jnp.where(masks == 1, 1.0, jnp.where(masks == 2, slope, 0.0))
        out_ref[1] = jnp.where(masks == 2, slope * lower, 0.0)


def interval(boxes, weight, bias, masks, spot):
    sites, _, images, cols = boxes.shape
    rows = weight.shape[0]
    return pl.pallas_call(
        interval_kernel,
        out_shape=jax.ShapeDtypeStruct((2, images, rows), F32),
        grid_spec=pltpu.PrefetchScalarGridSpec(
            num_scalar_prefetch=1,
            grid=(sites,),
            in_specs=[
                pl.BlockSpec((None, 2, images, cols), lambda i, spot: (spot[i], 0, 0, 0)),
                pl.BlockSpec((rows, cols), lambda i, spot: (0, i)),
                pl.BlockSpec((1, rows), lambda i, spot: (0, 0)),
                pl.BlockSpec((images, rows), lambda i, spot: (spot[sites], 0)),
            ],
            out_specs=pl.BlockSpec((2, images, rows), lambda i, spot: (0, 0, 0)),
            scratch_shapes=[pltpu.VMEM((rows, images), F32)] * 2,
        ),
        compiler_params=pltpu.CompilerParams(vmem_limit_bytes=VMEM_BYTES),
        cost_estimate=nothing(),
    )(spot, boxes, weight, bias, masks)


def scale_kernel(places, at_ref, slopes_ref, *refs):
    ow_refs, rest = refs[: len(places)], refs[len(places) :]
    at = at_ref[...]
    first = 0 if len(rest) == 1 else 3
    size = sum(shape[-2] for shape, _ in places)
    pick = (one_hot(at[:, first : first + 1], size) - one_hot(at[:, first + 1 : first + 2], size)).astype(BF16)
    coeff, low = None, 0
    for (shape, place), ref in zip(places, ow_refs):
        here = pick[:, low : low + shape[-2]]
        low += shape[-2]
        high_ow, low_ow = two_terms(ref[...] if place is None else ref[place])
        got = dot(here, high_ow) + dot(here, low_ow)
        coeff = got if coeff is None else coeff + got
    image = one_hot(at[:, 2:3], slopes_ref.shape[0]).astype(BF16)
    scaled = coeff * sum(dot(image, term) for term in three_terms(slopes_ref[...]))
    if first:
        offsets_ref, bias_ref, out_ref, relax_ref = rest
        offsets = sum(dot(image, term) for term in three_terms(offsets_ref[...]))
        relax_ref[...] = row_sums(scaled * bias_ref[...] - jnp.minimum(coeff, 0.0) * offsets)
    else:
        out_ref = rest[0]
    rows = scaled.shape[1]
    out_ref[:, :rows], out_ref[:, rows:] = two_terms(scaled)


def scale(at, ow_parts, slopes, *relax):
    specs, rows = at.shape[0], slopes.shape[1]
    outs = [jax.ShapeDtypeStruct((specs, 2 * rows), BF16)]
    if relax:
        outs = outs + [jax.ShapeDtypeStruct((8, specs), F32)]
    return pl.pallas_call(
        functools.partial(scale_kernel, [(array.shape, place) for array, place in ow_parts]),
        out_shape=outs,
        compiler_params=pltpu.CompilerParams(vmem_limit_bytes=VMEM_BYTES),
        cost_estimate=nothing(),
    )(at, slopes, *[array for array, _ in ow_parts], *relax)


def product_kernel(places, pieces, count, sum_places, *refs):
    col_ref, scaled_refs, refs = refs[0], refs[1 : count + 1], refs[count + 1 :]
    own_refs, refs = refs[: count * pieces - len(places)][:1], refs[min(1, count * pieces - len(places)) :]
    w_refs, refs = refs[: len(places)], refs[len(places) :]
    scaled_here, w_here, sems = refs[-3:]
    rows, piece = w_here.shape[1], w_here.shape[2] // pieces
    spans = [pl.ds(p * piece, piece) for p in range(pieces)]

    def columns(i):
        return pl.ds(pl.multiple_of(col_ref[i] * piece, piece), piece)

    sources = [ref.at[:, columns(p)] for ref in own_refs for p in range(pieces)]
    sources += [ref if where is None else ref.at[where] for ref, where in zip(w_refs, places)]
    copies = []

    def fetch(source, target):
        copies.append(pltpu.make_async_copy(source, target, sems.at[len(copies)]))
        copies[-1].start()

    for j in range(count):
        fetch(scaled_refs[j], scaled_here.at[j])
        for p in range(pieces):
            fetch(sources[j * pieces + p], w_here.at[j, :, spans[p]])
    operands = len(copies)
    if sum_places is not None:
        sums = len(sum_places)
        sum_refs, (near_ref, at_ref, margin_in) = refs[:sums], refs[sums : sums + 3]
        out_ref, margin_ref, block, near_here, sums_here = refs[-8:-3]
        for p in range(pieces):
            fetch(near_ref.at[:, :, columns(pieces + p)], near_here.at[:, :, spans[p]])
        for i, (ref, where) in enumerate(zip(sum_refs, sum_places)):
            (far, p, row), column = where
            target = sums_here.at[far, pl.ds(row, ref.shape[0]), spans[p]]
            fetch(ref.at[:, pl.ds(column * piece, piece)], target)
    total = None
    for j in range(count):
        for copy in copies[j * (pieces + 1) : (j + 1) * (pieces + 1)]:
            copy.wait()
        high, low = two_terms(w_here[j])
        got = dot(scaled_here[j], jnp.concatenate([high, high], axis=0)) + dot(scaled_here[j, :, :rows], low)
        total = got if total is None else total + got
    if sum_places is None:
        outs = refs[:-3]
        height = total.shape[0] // len(outs)
        for i, ref in enumerate(outs):
            ref[...] = total[i * height : (i + 1) * height]
        return
    for copy in copies[operands:]:
        copy.wait()
    for i in range(sums_here.shape[0]):
        total = total + sums_here[i]
    block[...] = total
    puts = []
    for p in range(pieces):
        puts.append(pltpu.make_async_copy(block.at[:, spans[p]], out_ref.at[:, columns(pieces + p)], sems.at[p]))
        puts[-1].start()
    image = one_hot(at_ref[...][:, 5:6], near_here.shape[1]).astype(BF16)
    center = sum(dot(image, term) for term in three_terms(near_here[0]))
    radius = sum(dot(image, term) for term in three_terms(near_here[1]))
    margin_ref[...] = margin_in[...] + row_sums(total * center - jnp.abs(total) * radius)
    for put in puts:
        put.wait()


def product(scaled, weight, col, w_parts, split=1, final=None):
    specs, rows = scaled[0].shape[0], scaled[0].shape[1] // 2
    piece = w_parts[0][0].shape[-1]
    pieces = col.shape[0] // 2
    weight = [weight] if len(w_parts) < len(scaled) * pieces else []
    whole = pl.BlockSpec(memory_space=pltpu.VMEM)
    there = pl.BlockSpec(memory_space=pl.ANY if len(scaled) == 1 else pltpu.HBM)
    args = [col, *scaled, *weight, *[array for array, _ in w_parts]]
    in_specs = [pl.BlockSpec(memory_space=pltpu.SMEM)] + [there] * (len(args) - 1)
    scratch, n_sems = [], (1 + pieces) * len(scaled)
    aliases, sum_places = {}, None
    if final is None:
        out_shape, out_specs = [jax.ShapeDtypeStruct((specs // split, pieces * piece), F32)] * split, [whole] * split
    else:
        sum_parts, at, near, margin, out = final
        sums, sum_places = len(sum_parts), [where for _, where in sum_parts]
        in_specs += [there] * (sums + 1) + [whole] * 2
        args += [*[array for array, _ in sum_parts], near, at, margin]
        if out is not None:
            aliases = {len(args): 0}
            in_specs.append(there)
            args.append(out)
        out_shape = [jax.ShapeDtypeStruct((specs, QUARTERS * piece), F32), jax.ShapeDtypeStruct((8, specs), F32)]
        out_specs = [there, whole]
        scratch = [
            pltpu.VMEM((specs, pieces * piece), F32),
            pltpu.VMEM((2, near.shape[1], pieces * piece), F32),
            pltpu.VMEM((1 + max(where[0][0] for where in sum_places), specs, pieces * piece), F32),
        ]
        n_sems += pieces + sums
    scratch += [
        pltpu.VMEM((len(scaled), specs, 2 * rows), BF16),
        pltpu.VMEM((len(scaled), rows, pieces * piece), F32),
        pltpu.SemaphoreType.DMA((n_sems,)),
    ]
    return pl.pallas_call(
        functools.partial(product_kernel, [place for _, place in w_parts], pieces, len(scaled), sum_places),
        out_shape=out_shape,
        in_specs=in_specs,
        out_specs=out_specs,
        scratch_shapes=scratch,
        input_output_aliases=aliases,
        compiler_params=pltpu.CompilerParams(vmem_limit_bytes=MORE_VMEM_BYTES if weight else VMEM_BYTES),
        cost_estimate=nothing(),
    )(*args)


class Rounds:
    def __init__(self):
        self.got, self.fresh = {}, []

    def keep(self, name, value):
        self.got[name] = value
        self.fresh.append(name)

    def edge(self, *sends, only=None):
        names = self.fresh if only is None else only
        held = [self.got[name] for name in names]
        done = lax.optimization_barrier((*[value for _, value, _ in sends], *held))
        self.got.update(zip(names, done[len(sends) :]))
        self.fresh = [name for name in self.fresh if name not in names]
        for (name, _, move), value in zip(sends, done):
            self.keep(name, move(value))

    def send(self, name, value, move):
        self.keep(name, move(value))


def local(members, sites, center, radius, weight, bias, out_weight, masks, image_labels, runner_up, spec_image):
    g, n = lax.axis_index("spec"), lax.axis_index("neuron")
    q = g % QUARTERS
    rows, cols = weight.shape[0], center.shape[1]
    images, classes = center.shape[0], out_weight.shape[0]
    piece = cols // QUARTERS
    cut = sites // 2
    pair = 2
    group = (pair, cut, cut + pair)
    targets = [m for m in range(1, sites) if not m & (cut + pair)] + [0]

    def to_site(k):
        return functools.partial(swap, axis="neuron", size=sites, k=k)

    def to_member(k):
        return functools.partial(swap, axis="spec", size=members, k=k)

    work = Rounds()
    got, keep, edge, send = work.got, work.keep, work.edge, work.send
    where = {}

    share = -(-classes // QUARTERS // 8) * 8

    def start_of(part):
        return jnp.minimum(part * share, classes - share)

    def columns(t, j):
        block = lax.dynamic_slice(weight, (0, (n ^ j ^ t) * cols + q * piece), (rows, piece))
        where[t, j, 0] = (t, j, 0), None
        return (t, j, 0), block, to_site(j)

    def part(name):
        key, place = where[name]
        return got[key], place

    def value(name):
        array, place = part(name)
        return array if place is None else array[place]

    def share_out(k, *names):
        pieces = [value(name) for name in names]
        names = [(what, j, r ^ k) for what, j, r in names]
        if len(names) == 1:
            where[names[0]] = names[0], None
            return names[0], pieces[0], to_member(k)
        for i, name in enumerate(names):
            where[name] = tuple(names), i
        return tuple(names), jnp.stack(pieces), to_member(k)

    ow = lax.dynamic_slice(out_weight, (start_of(q), 0), (share, rows))
    for j in group:
        where["ow", j, 0] = ("ow", j, 0), None
    t = targets[0]
    near = jnp.stack([center, radius])
    boxes = near[None]
    order = [0]
    k = cut
    while k:
        if k == 1:
            keep("boxes", boxes)
            edge((("ow", cut, 0), ow, to_site(cut)), (("ow", pair, 0), ow, to_site(pair)), only=["boxes"])
            boxes = got["boxes"]
        boxes = jnp.concatenate([boxes, to_site(k)(boxes)])
        order = order + [o ^ k for o in order]
        k //= 2
    keep("boxes", boxes)
    k = 1
    while k < members:
        near = jnp.concatenate([near, to_member(k)(near)], axis=1)
        k *= 2
    keep("near", near)
    spot = jnp.zeros((sites,), jnp.int32)
    for s, o in enumerate(order):
        spot = jnp.where((n ^ jnp.arange(sites)) == o, s, spot)

    edge(columns(t, cut))
    send(("ow", cut + pair, 0), got["ow", cut, 0], to_site(pair))
    send(*share_out(2, ("ow", pair, 0)))
    send(*share_out(2, ("ow", cut, 0)))
    both = interval(got["boxes"], weight, bias[None], masks, jnp.append(spot, g))
    keep("both", lax.all_gather(both, "spec", axis=1, tiled=True))
    labels = jnp.sum(jnp.where(spec_image[:, None] == jnp.arange(image_labels.shape[0]), image_labels, 0), axis=1)

    def place(label):
        part = label // share
        return (part ^ q) * share + label - start_of(part)

    near_image = ((spec_image // images) ^ g) * images + spec_image % images
    keep("at", jnp.stack([place(labels), place(runner_up), spec_image, labels, runner_up, near_image], axis=1))

    edge(columns(t, cut + pair), columns(t, pair))
    send(*share_out(2, ("ow", cut + pair, 0)))
    send(*share_out(2, (t, cut, 0)))
    slopes, offsets = got["both"][0], got["both"][1]
    slopes = jnp.stack([slopes, to_site(pair)(slopes)])
    slopes = jnp.concatenate([slopes, to_site(cut)(slopes)])
    keep("slopes", slopes)
    slopes = slopes[0]
    scaled, margin = scale(got["at"], [(out_weight, None)], slopes, offsets, bias[None])
    keep("margin", margin)
    keep(("scaled", 0), scaled)

    sum_parts = {}

    def some_product(t, *members_at, sites=(0, *group), last=True):
        parts = [part((t, j, r)) for j in sites if j for r in members_at]
        col = jnp.stack([(n ^ t) * QUARTERS + (q ^ r) for r in members_at] + [q ^ r for r in members_at])
        scaled = [got["scaled", j] for j in sites]
        if t or not last:
            (made,) = product(scaled, weight, col, parts)
            keep(("product", t, members_at), made)
            return
        had = []
        for i, f in enumerate(targets):
            for p, r in enumerate(members_at):
                if f:
                    had.append((got["sum", f, members_at], ((i, p, 0), p)))
                elif len(sites) <= len(group):
                    had.append((got["product", t, members_at], ((i, p, 0), p)))
        final = had, got["at"], got["near"], got["margin"], got.get("out")
        out, margin = product(scaled, weight, col, parts, final=final)
        keep("out", out)
        keep("margin", margin)

    def send_sum(t, *members_at):
        send(("sum", t, members_at), got["product", t, members_at], to_site(t))

    for i, t in enumerate(targets):
        after = targets[i + 1 :][:1]
        edge(*([columns(after[0], cut), columns(after[0], pair)] if after else []))
        if i:
            send_sum(targets[i - 1], 2, 3)
        else:
            slopes = got["slopes"]
        if i == 0:
            send(*share_out(2, (t, pair, 0)))
        send(*share_out(2, (t, cut + pair, 0)))
        if t:
            send(*share_out(1, *[(t, j, 0) for j in group]))
        else:
            send(*share_out(1, (t, pair, 0), (t, cut, 0)))
            send(*share_out(1, (t, cut + pair, 0)))
            send(*share_out(1, (t, pair, 2)))
            send(*share_out(1, (t, cut, 2)))
        if i == 0:
            send(*share_out(1, *[("ow", j, r) for j in group for r in (0, 2)]))
            for j, slot in ((pair, 1), (cut, 2), (cut + pair, 3)):
                parts = [part(("ow", j, r)) for r in range(QUARTERS)]
                (got["scaled", j],) = scale(got["at"], parts, slopes[slot])
        some_product(t, 0, 1)
        if not t:
            some_product(t, 2, 3, sites=(0, pair, cut), last=False)
        names = [name for name in work.fresh if name[0] != "sum" or t]
        edge(*([columns(after[0], cut + pair)] if after else []), only=names)
        if after:
            send(*share_out(2, (after[0], cut, 0)))
            send(*share_out(2, (after[0], pair, 0)))
        if t:
            send(*share_out(1, *[(t, j, 2) for j in group]))
            send_sum(t, 0, 1)
            some_product(t, 2, 3)
        else:
            send(*share_out(1, (t, cut + pair, 2)))
            some_product(t, 2, 3, sites=(cut + pair,))
    out, margin = got["out"], got["margin"]
    margin = margin + (to_site(1)(margin) + to_site(2)(margin) + to_site(3)(margin))
    k = 4
    while k < sites:
        margin = margin + to_site(k)(margin)
        k *= 2
    return out, margin[0]


def solution(mesh):
    members, sites = mesh.shape["spec"], mesh.shape["neuron"]
    return jax.shard_map(
        functools.partial(local, members, sites),
        mesh=mesh,
        in_specs=(
            P("spec", "neuron"),
            P("spec", "neuron"),
            P("neuron", None),
            P("neuron"),
            P(None, "neuron"),
            P(None, "neuron"),
            P(),
            P("spec"),
            P("spec"),
        ),
        out_specs=(P("spec", "neuron"), P("spec")),
        check_vma=False,
    )
```
